128 devices in a mesh: ctx: 16 (over x_lo, y, core), exp: 8 (over x_hi, z).
Axes of the slice: x: 4 (x_hi: 2, x_lo: 2; x = x_hi * 2 + x_lo), y: 4, z: 4, core: 2. Of those that a mesh axis runs over, the one named last changes fastest.
Arguments:
- queries: bfloat16 [2048, 4096], P('ctx', 'exp'), may hold values from -8 to 8
- new_keys: bfloat16 [2048, 1024], P('ctx', 'exp'), may hold values from -6 to 6
- new_values: bfloat16 [2048, 1024], P('ctx', 'exp'), may hold values from -6 to 6
- cache_keys: bfloat16 [16384, 1024], P('ctx', 'exp'), may hold values from -8 to 8
- cache_values: bfloat16 [16384, 1024], P('ctx', 'exp'), may hold values from -6 to 6
- cache_length: int32 [1], replicated, may hold values from 12288 to 16384
- residual: bfloat16 [2048, 4096], P(('ctx', 'exp')), may hold values from -6 to 6
- out_weight: bfloat16 [4096, 4096], P('exp'), may hold values from -0.5 to 0.5
- norm_gain: bfloat16 [4096], replicated, may hold values from 0.5 to 1.5
- route_ids: int32 [2048, 2], P('ctx'), may hold values from 0 to 7, all different within a row; in each aligned block of 128 rows (0 to 127, 128 to 255, ...) at most 48 rows name the same one
- route_gates: float32 [2048, 2], P('ctx'), may hold values from 0.2 to 1
- w_gate: bfloat16 [8, 4096, 14336], P('exp', None, 'ctx'), may hold values from -0.09375 to 0.09375
- w_up: bfloat16 [8, 4096, 14336], P('exp', None, 'ctx'), may hold values from -0.09375 to 0.09375
- w_down: bfloat16 [8, 14336, 4096], P('exp', 'ctx'), may hold values from -0.046875 to 0.046875
Outputs:
- layer_out: bfloat16 [2048, 4096], P(('ctx', 'exp'))
The draws below stay inside these ranges and needn't reach their ends.
Inputs may be any that keep to these rules, and one draw needn't show every extreme that they name: `route_ids`: each row names 2 different experts; in each aligned block of 128 rows no expert is named more than 48 times, and in some block one expert is named exactly 48 times.
All inputs are finite; a program needn't handle non-finite values.
Results may differ from the reference program's by a relative error of at most 0.024.
Values may be sent and summed in bfloat16 or wider, within the bound.
A program may use at most 128 MiB of HBM per device.

```python
import math
import jax
import jax.numpy as jnp
import numpy as np
from jax import lax

D = 4096
FF = 14336
HEADS = 32
KV_HEADS = 8
HD = 128
TOP = 2
TOK_DEV = 128
TOKENS = 2048
CACHE = 16384
EXPERTS = 8
CAP = 48
N_CTX = 16


def draw_queries(key, part):
    key = jax.random.fold_in(key, 11)
    values = jnp.clip(jax.random.normal(key, (TOKENS, HEADS * HD), jnp.float32), -6.0, 6.0)
    return values.astype(jnp.bfloat16)


def draw_cache_keys(key, part):
    key = jax.random.fold_in(key, 23)
    values = jnp.clip(jax.random.normal(key, (CACHE, KV_HEADS * HD), jnp.float32), -6.0, 6.0)
    return values.astype(jnp.bfloat16)


def level_of(own_key, extent, cuts, low, high):
    gain, own = 1.0, jax.random.fold_in(own_key, 6)
    for axis_at, blocks in cuts:
        draws = jnp.exp(jax.random.uniform(jax.random.fold_in(own, axis_at), (blocks,), jnp.float32, low / len(cuts), high / len(cuts)))
        gain = gain * jnp.repeat(draws, extent[axis_at] // blocks).reshape([-1 if axis == axis_at else 1 for axis in range(len(extent))])
    return gain


def shared_out(rng, own, number, rows, number_of, top, most, lean):
    sequence = jax.random.permutation(rng, number_of)
    packed, common = portions_of(number_of, rows * top, most, lean, True), portions_of(number_of, rows * top, most, lean, False)
    places = jnp.arange(number_of)

    def named(lengths, turn):
        used = int((lengths > 0).sum())
        fixed = max(1, used // 4)
        shifted = fixed + (places - fixed + turn * (used - fixed)) % max(1, number_of - fixed)
        return jnp.zeros((number_of,), jnp.int32).at[sequence[jnp.where(places < fixed, places, shifted)]].set(jnp.asarray(lengths, jnp.int32))

    lengths = jnp.where(number % 4 == 0, named(packed, number // 4), named(common, number - number // 4 - 1))
    mixed = jax.random.permutation(jax.random.fold_in(own, 3), number_of)
    giver, sink = mixed[0:number_of // 2 * 2:2], mixed[1:number_of // 2 * 2:2]
    slack = jnp.minimum(lengths[giver] - 1, most - lengths[sink]) // 2
    slack = jnp.where((giver == sequence[0]) | (sink == sequence[0]) | (lengths[sink] == 0), 0, jnp.maximum(slack, 0))
    shifted = jax.random.randint(jax.random.fold_in(own, 4), (number_of // 2,), 0, 1 << 20) % (slack + 1)
    lengths = lengths.at[giver].add(-shifted).at[sink].add(shifted)
    members = jnp.searchsorted(jnp.cumsum(lengths), jnp.arange(rows * top), side="right").astype(jnp.int32)
    table = members.reshape(top, rows).T
    table = table[jax.random.permutation(jax.random.fold_in(own, 1), rows)]
    turn = jax.random.randint(jax.random.fold_in(own, 2), (rows, 1), 0, top)
    return jnp.take_along_axis(table, (jnp.arange(top)[None, :] + turn) % top, axis=1)


def portions_of(count, total, reach, lean, full):
    weights = [(1 << 20) // math.isqrt(standing ** lean) + 1 for standing in range(1, count + 1)]
    largest = reach if full else min(reach, max(-(-total // count), total * weights[0] // sum(weights)))
    least = 1 if total - largest >= count - 1 else 0
    counts, spare = [largest] + [least] * (count - 1), total - largest - least * (count - 1)
    while spare > 0:
        movable = [i for i in range(1, count) if counts[i] < largest] or [i for i in range(1, count) if counts[i] < reach]
        mass, budget = sum([weights[i] for i in movable]), spare
        for i in movable:
            addition = min(reach - counts[i], max(1, budget * weights[i] // mass), spare)
            counts[i] = counts[i] + addition
            spare = spare - addition
    return np.array(counts)


def noise(stream_key, dims, scale, most, shards=(), kind=jnp.bfloat16):
    level = level_of(stream_key, dims, shards, -0.22, 0.18) if shards else 1.0
    values = jax.random.normal(stream_key, dims, jnp.float32) * scale * level
    return jnp.minimum(jnp.maximum(values, -most), most).astype(kind)


def setup_inputs(seed: int = 0) -> dict:
    keys = jax.random.split(jax.random.key(seed), 15)
    queries = draw_queries(jax.random.fold_in(keys[14], 71), 0)
    new_keys = noise(keys[1], (TOKENS, KV_HEADS * HD), 1.0, 6.0, ((0, 16), (1, 8)))
    new_values = noise(keys[2], (TOKENS, KV_HEADS * HD), 1.0, 6.0, ((0, 16), (1, 8)))
    cache_keys = draw_cache_keys(jax.random.fold_in(keys[14], 71), 0)
    cache_values = noise(keys[4], (CACHE, KV_HEADS * HD), 1.0, 6.0, ((0, 16), (1, 8)))
    cache_length = jax.random.randint(keys[5], (1,), CACHE * 3 // 4, CACHE + 1).astype(jnp.int32)
    residual = noise(keys[6], (TOKENS, D), 1.0, 6.0, ((0, 128),))
    out_weight = noise(keys[7], (HEADS * HD, D), HD ** -0.5, 0.5, ((0, 8),))
    norm_gain = jnp.clip(1.0 + 0.1 * jax.random.normal(keys[8], (D,), jnp.float32), 0.5, 1.5).astype(jnp.bfloat16)
    route_ids_keys = jax.random.split(jax.random.fold_in(keys[9], 1), TOKENS // TOK_DEV)
    route_ids_turns = jax.random.permutation(jax.random.fold_in(keys[9], 3), TOKENS // TOK_DEV)
    route_ids = jax.vmap(lambda own, number: shared_out(jax.random.fold_in(keys[9], 2), own, number, TOK_DEV, EXPERTS, TOP, CAP, 2))(route_ids_keys, route_ids_turns).reshape((TOKENS, TOP))
    route_gates = jnp.clip(0.2 + 0.8 * jax.random.uniform(keys[10], (TOKENS, TOP), jnp.float32) ** level_of(keys[10], (TOKENS, TOP), ((0, 16),), -0.2, 0.2), 0.2, 1.0)
    w_gate = noise(keys[11], (EXPERTS, D, FF), D ** -0.5, 0.09375, ((0, 8), (2, 16)))
    w_up = noise(keys[12], (EXPERTS, D, FF), D ** -0.5, 0.09375, ((0, 8), (2, 16)))
    w_down = noise(keys[13], (EXPERTS, FF, D), FF ** -0.5, 0.046875, ((0, 8), (1, 16)))
    return dict(queries=queries, new_keys=new_keys, new_values=new_values, cache_keys=cache_keys, cache_values=cache_values, cache_length=cache_length, residual=residual, out_weight=out_weight, norm_gain=norm_gain, route_ids=route_ids, route_gates=route_gates, w_gate=w_gate, w_up=w_up, w_down=w_down)


EPS = 1e-05

def reference(queries, new_keys, new_values, cache_keys, cache_values, cache_length, residual, out_weight, norm_gain, route_ids, route_gates, w_gate, w_up, w_down):
    group = HEADS // KV_HEADS
    scale = 1.0 / math.sqrt(HD)
    limit = cache_length[0]
    key_rows = CACHE + TOKENS
    keys_all = jnp.concatenate([cache_keys, new_keys], 0).reshape(key_rows, KV_HEADS, HD).astype(jnp.float32)
    values_all = jnp.concatenate([cache_values, new_values], 0).reshape(key_rows, KV_HEADS, HD).astype(jnp.float32)
    row_index = jnp.arange(key_rows, dtype=jnp.int32)
    in_cache = row_index < CACHE
    heads_q = queries.reshape(TOKENS // TOK_DEV, TOK_DEV, KV_HEADS, group, HD)

    def attend_block(block_id):
        query_block = lax.dynamic_index_in_dim(heads_q, block_id, 0, keepdims=False).astype(jnp.float32)
        query_index = block_id * TOK_DEV + jnp.arange(TOK_DEV, dtype=jnp.int32)
        visible = jnp.where(in_cache[None, :], (row_index < limit)[None, :], (row_index - CACHE)[None, :] <= query_index[:, None])

        def one_head(head_id):
            query_head = lax.dynamic_index_in_dim(query_block, head_id, 1, keepdims=False)
            key_head = lax.dynamic_index_in_dim(keys_all, head_id, 1, keepdims=False)
            value_head = lax.dynamic_index_in_dim(values_all, head_id, 1, keepdims=False)
            scores = jnp.einsum('qgd,rd->gqr', query_head, key_head) * scale
            scores = jnp.where(visible[None], scores, -jnp.inf)
            largest = lax.optimization_barrier(jnp.max(scores, -1, keepdims=True))
            weights = jnp.where(visible[None], jnp.exp(scores - largest), 0.0)
            totals = lax.optimization_barrier(jnp.sum(weights, -1))
            rounded = lax.optimization_barrier(weights.astype(jnp.bfloat16)).astype(jnp.float32)
            summed = jnp.einsum('gqr,rd->qgd', rounded, value_head)
            return summed / jnp.transpose(totals)[:, :, None]
        per_head = lax.map(one_head, jnp.arange(KV_HEADS, dtype=jnp.int32))
        return jnp.transpose(per_head, (1, 0, 2, 3)).reshape(TOK_DEV, HEADS * HD)
    attended = lax.map(attend_block, jnp.arange(TOKENS // TOK_DEV, dtype=jnp.int32))
    attended = attended.reshape(TOKENS, HEADS * HD).astype(jnp.bfloat16)
    mixed = residual.astype(jnp.float32) + jnp.dot(attended, out_weight, preferred_element_type=jnp.float32)
    mean_square = lax.optimization_barrier(jnp.mean(mixed * mixed, -1, keepdims=True))
    normed = (mixed * lax.rsqrt(mean_square + EPS) * norm_gain.astype(jnp.float32)).astype(jnp.bfloat16)
    flat_ids = route_ids.reshape(-1)
    capacity_all = N_CTX * CAP
    ff_block = FF // N_CTX

    def run_expert(inputs):
        expert_id, gate_mat, up_mat, down_mat = inputs
        chosen = jnp.nonzero(flat_ids == expert_id, size=capacity_all, fill_value=TOKENS * TOP)[0].astype(jnp.int32)
        token_rows = jnp.minimum(chosen // TOP, TOKENS - 1)
        picked = jnp.take(normed, token_rows, axis=0)
        gate_part = jnp.dot(picked, gate_mat, preferred_element_type=jnp.float32)
        up_part = jnp.dot(picked, up_mat, preferred_element_type=jnp.float32)
        hidden = (jax.nn.silu(gate_part) * up_part).astype(jnp.bfloat16)
        parts = jnp.einsum('rcf,cfd->crd', hidden.reshape(capacity_all, N_CTX, ff_block).astype(jnp.float32), down_mat.reshape(N_CTX, ff_block, D).astype(jnp.float32))
        rounded = lax.optimization_barrier(parts.astype(jnp.bfloat16)).astype(jnp.float32)
        return (chosen, lax.optimization_barrier(jnp.sum(rounded, 0)).astype(jnp.bfloat16))
    chosen_all, outputs = lax.map(run_expert, (jnp.arange(EXPERTS, dtype=jnp.int32), w_gate, w_up, w_down))
    per_slot = jnp.zeros((TOKENS * TOP, D), jnp.float32).at[chosen_all.reshape(-1)].set(outputs.reshape(-1, D).astype(jnp.float32), mode='drop')
    experts_sum = lax.optimization_barrier(jnp.sum(route_gates[:, :, None] * per_slot.reshape(TOKENS, TOP, D), 1))
    return (mixed + experts_sum).astype(jnp.bfloat16)
```

```python
import math

import jax
import jax.numpy as jnp
from jax import lax
from jax.sharding import PartitionSpec as P

HD = 128


NEG = -1e30
EPS = 1e-05
BLOCK_ROWS = 1024


def attend_piece(
    carry,
    query_block,
    query_index,
    key_piece,
    value_piece,
    start,
    cache_rows,
    new_rows,
    cache_limit,
):
    shard_rows = cache_rows + new_rows
    kv_local = key_piece.shape[1] // HD
    group = query_block.shape[1] // key_piece.shape[1]
    heads_q = query_block.reshape(query_block.shape[0], kv_local, group, HD)
    count = key_piece.shape[0]
    width = min(count, BLOCK_ROWS)
    blocks = -(-count // width)
    keys_padded = key_piece.reshape(blocks, width, kv_local, HD)
    values_padded = value_piece.reshape(blocks, width, kv_local, HD)
    block_start = width * jnp.arange(blocks, dtype=jnp.int32)
    scale = 1.0 / math.sqrt(HD)

    def step_block(state, inputs):
        top, total, summed = state
        keys_block, values_block, first_row = inputs
        row_index = first_row + jnp.arange(width, dtype=jnp.int32)
        shard = row_index // shard_rows
        offset = row_index % shard_rows
        cache_pos = shard * cache_rows + offset
        new_pos = shard * new_rows + offset - cache_rows
        visible = jnp.where(
            (offset < cache_rows)[None, :],
            (cache_pos < cache_limit)[None, :],
            new_pos[None, :] <= query_index[:, None],
        )
        visible = visible & (row_index < start + count)[None, :]
        scores = (
            jnp.einsum("qkgd,rkd->kgqr", heads_q, keys_block, preferred_element_type=jnp.float32)
            * scale
        )
        scores = jnp.where(visible[None, None], scores, NEG)
        top_new = jnp.maximum(top, jnp.max(scores, -1))
        weights = jnp.where(visible[None, None], jnp.exp(scores - top_new[..., None]), 0.0)
        shrink = jnp.exp(top - top_new)
        total = total * shrink + jnp.sum(weights, -1)
        summed = summed * shrink[..., None] + jnp.einsum(
            "kgqr,rkd->kgqd",
            weights.astype(jnp.bfloat16),
            values_block,
            preferred_element_type=jnp.float32,
        )
        return ((top_new, total, summed), None)

    state, unused = lax.scan(step_block, carry, (keys_padded, values_padded, block_start))
    return state


def local(
    queries,
    new_keys,
    new_values,
    cache_keys,
    cache_values,
    cache_length,
    residual,
    out_weight,
    norm_gain,
    route_ids,
    route_gates,
    w_gate,
    w_up,
    w_down,
):
    tok_rows = queries.shape[0]
    cache_rows = cache_keys.shape[0]
    ctx_index = lax.axis_index("ctx")
    exp_index = lax.axis_index("exp")
    cache_limit = cache_length[0]
    local_keys = jnp.concatenate([cache_keys, new_keys], 0)
    local_values = jnp.concatenate([cache_values, new_values], 0)
    kv_local = cache_keys.shape[1] // HD
    group = queries.shape[1] // cache_keys.shape[1]
    heads_local = kv_local * group
    initial = (
        jnp.full((kv_local, group, tok_rows), NEG, jnp.float32),
        jnp.zeros((kv_local, group, tok_rows), jnp.float32),
        jnp.zeros((kv_local, group, tok_rows, HD), jnp.float32),
    )
    query_index = ctx_index * tok_rows + jnp.arange(tok_rows, dtype=jnp.int32)
    top, total, summed = attend_piece(
        initial,
        queries,
        query_index,
        lax.all_gather(local_keys, "ctx", axis=0, tiled=True),
        lax.all_gather(local_values, "ctx", axis=0, tiled=True),
        jnp.int32(0),
        cache_rows,
        tok_rows,
        cache_limit,
    )
    attended = (
        (summed / total[..., None])
        .transpose(2, 0, 1, 3)
        .reshape(tok_rows, heads_local * HD)
        .astype(jnp.bfloat16)
    )
    projected = jnp.dot(attended, out_weight, preferred_element_type=jnp.float32)
    sub_rows = residual.shape[0]
    own_first = exp_index * sub_rows
    placed = lax.dynamic_update_slice_in_dim(
        jnp.zeros_like(projected), residual.astype(jnp.float32), own_first, 0
    )
    mixed = lax.psum((projected + placed).astype(jnp.bfloat16), "exp").astype(jnp.float32)
    mean_square = jnp.mean(mixed * mixed, -1, keepdims=True)
    normed = (mixed * lax.rsqrt(mean_square + EPS) * norm_gain.astype(jnp.float32)).astype(
        jnp.bfloat16
    )
    capacity = 3 * tok_rows // lax.axis_size("exp")
    hits = route_ids == exp_index
    row_hit = jnp.any(hits, 1)
    order = jnp.arange(tok_rows, dtype=jnp.int32)
    earlier = row_hit[None, :] & (order[None, :] <= order[:, None])
    slot = jnp.sum(earlier.astype(jnp.int32), 1) - 1
    select = (
        (slot[None, :] == jnp.arange(capacity, dtype=jnp.int32)[:, None]) & row_hit[None, :]
    ).astype(jnp.bfloat16)
    outgoing = jnp.dot(select, normed, preferred_element_type=jnp.float32).astype(jnp.bfloat16)
    gate_local = w_gate[0]
    up_local = w_up[0]
    down_local = w_down[0]
    piece = lax.all_gather(outgoing, "ctx", axis=0, tiled=True)
    gate_part = jnp.dot(piece, gate_local, preferred_element_type=jnp.float32)
    up_part = jnp.dot(piece, up_local, preferred_element_type=jnp.float32)
    hidden = (jax.nn.silu(gate_part) * up_part).astype(jnp.bfloat16)
    terms = jnp.dot(hidden, down_local, preferred_element_type=jnp.float32)
    expert_out = lax.psum_scatter(
        terms.astype(jnp.bfloat16), "ctx", scatter_dimension=0, tiled=True
    )
    returned = jnp.dot(jnp.transpose(select), expert_out, preferred_element_type=jnp.float32)
    weight_row = jnp.sum(jnp.where(hits, route_gates, 0.0), 1)
    weighted = weight_row[:, None] * returned
    combined = lax.psum_scatter(
        weighted.astype(jnp.bfloat16), "exp", scatter_dimension=0, tiled=True
    ).astype(jnp.float32)
    own_mixed = lax.dynamic_slice_in_dim(mixed, own_first, sub_rows, 0)
    return (own_mixed + combined).astype(jnp.bfloat16)


def solution(mesh):
    placed = (
        P("ctx", "exp"),
        P("ctx", "exp"),
        P("ctx", "exp"),
        P("ctx", "exp"),
        P("ctx", "exp"),
        P(),
        P(("ctx", "exp"), None),
        P("exp", None),
        P(),
        P("ctx", None),
        P("ctx", None),
        P("exp", None, "ctx"),
        P("exp", None, "ctx"),
        P("exp", "ctx", None),
    )
    return jax.shard_map(
        local, mesh=mesh, in_specs=placed, out_specs=P(("ctx", "exp"), None), check_vma=False
    )
```

```python
import functools
import math

import jax
import jax.numpy as jnp
from jax import lax
from jax.experimental import pallas as pl
from jax.experimental.pallas import tpu as pltpu
from jax.sharding import PartitionSpec as P

HD = 128
NEG = -1e30
EPS = 1e-05
MESH = pl.DeviceIdType.MESH
F32 = jnp.float32
BF16 = jnp.bfloat16


def remote(src, dst, send, recv, where):
    return pltpu.make_async_remote_copy(
        src_ref=src,
        dst_ref=dst,
        send_sem=send,
        recv_sem=recv,
        device_id=where,
        device_id_type=MESH,
    )


def attend_kernel(
    n_ctx,
    n_exp,
    limit_ref,
    q_ref,
    nk_ref,
    nv_ref,
    ck_ref,
    cv_ref,
    res_ref,
    ow_ref,
    gain_ref,
    sel_ref,
    out_ref,
    mixed_ref,
    kbuf,
    vbuf,
    kt,
    vext,
    qbuf,
    osend,
    orecv,
    ssend,
    srecv,
    att,
    ow_v,
    psend,
    precv,
    nbuf,
    kv_send,
    kv_recv,
    q_send,
    q_recv,
    o_send,
    o_recv,
    s_send,
    s_recv,
    p_send,
    p_recv,
    n_send,
    n_recv,
    ow_sem,
):
    n_chip = n_ctx // 2
    me = lax.axis_index("ctx")
    ex = lax.axis_index("exp")
    chip = me // 2
    core = me % 2
    sib = me + 1 - 2 * core
    tok = q_ref.shape[0]
    group = q_ref.shape[1] // HD
    cache = ck_ref.shape[0]
    width = res_ref.shape[1]
    sub = res_ref.shape[0]
    c_all = 2 * cache
    rows = c_all + 2 * tok

    ow_copy = pltpu.make_async_copy(ow_ref, ow_v, ow_sem)
    ow_copy.start()

    barrier = pltpu.get_barrier_semaphore()

    def greet_chip(s, _):
        peer = ((chip + s) % n_chip) * 2 + core
        pl.semaphore_signal(barrier, inc=1, device_id={"ctx": peer}, device_id_type=MESH)
        return 0

    def greet_exp(s, _):
        pl.semaphore_signal(
            barrier, inc=1, device_id={"exp": (ex + s) % n_exp}, device_id_type=MESH
        )
        return 0

    pl.semaphore_signal(barrier, inc=1, device_id={"ctx": sib}, device_id_type=MESH)
    lax.fori_loop(1, n_chip, greet_chip, 0)
    lax.fori_loop(1, n_exp, greet_exp, 0)

    for g in range(group):
        qbuf[chip, g * tok : (g + 1) * tok, :] = q_ref[:, g * HD : (g + 1) * HD]
    kbuf[0:cache, :] = ck_ref[...]
    kbuf[c_all : c_all + tok, :] = nk_ref[...]
    vbuf[0:cache, :] = cv_ref[...]
    vbuf[c_all : c_all + tok, :] = nv_ref[...]

    pl.semaphore_wait(barrier, n_chip + n_exp - 1)

    kv_copies = [
        remote(src, dst, kv_send.at[i], kv_recv.at[i], {"ctx": sib})
        for i, (src, dst) in enumerate(
            [
                (ck_ref, kbuf.at[pl.ds(cache, cache)]),
                (nk_ref, kbuf.at[pl.ds(c_all + tok, tok)]),
                (cv_ref, vbuf.at[pl.ds(cache, cache)]),
                (nv_ref, vbuf.at[pl.ds(c_all + tok, tok)]),
            ]
        )
    ]
    for copy in kv_copies:
        copy.start()

    def q_copy(s):
        peer = ((chip + n_chip - s) % n_chip) * 2 + core
        return remote(
            qbuf.at[chip], qbuf.at[chip], q_send.at[s], q_recv.at[chip], {"ctx": peer}
        )

    def q_start(s, _):
        q_copy(s).start()
        return 0

    lax.fori_loop(1, n_chip, q_start, 0)

    for copy in kv_copies:
        copy.wait_recv()
    kt[...] = kbuf[...].T
    vext[:, 0:HD] = vbuf[...]
    vext[:, HD : 2 * HD] = jnp.ones((rows, HD), BF16)

    limit = limit_ref[0]
    position = lax.broadcasted_iota(jnp.int32, (1, cache), 1)
    bias_own = jnp.where(position + me * cache < limit, 0.0, NEG)
    bias_sib = jnp.where(position + sib * cache < limit, 0.0, NEG)
    cache_bias = jnp.concatenate([bias_own, bias_sib], axis=1)
    t_row = lax.broadcasted_iota(jnp.int32, (tok, 2 * tok), 0)
    t_col = lax.broadcasted_iota(jnp.int32, (tok, 2 * tok), 1)
    lane = lax.broadcasted_iota(jnp.int32, (tok, HD), 1)
    key_at = jnp.where(t_col < tok, t_col + me * tok, t_col - tok + sib * tok)
    scale = math.log2(math.e) / math.sqrt(HD)

    def o_copy(s, src):
        peer = src * 2 + core
        return (
            remote(osend.at[s], orecv.at[chip], o_send.at[s], o_recv.at[chip], {"ctx": peer}),
            remote(ssend.at[s], srecv.at[chip], s_send.at[s], s_recv.at[chip], {"ctx": peer}),
        )

    def step(s, _):
        src = (chip + s) % n_chip

        @pl.when(s > 0)
        def _():
            remote(
                qbuf.at[src], qbuf.at[src], q_send.at[s], q_recv.at[src], {"ctx": src * 2 + core}
            ).wait_recv()

        query_at = t_row + (src * 2 + core) * tok
        new_bias = jnp.where(key_at <= query_at, 0.0, NEG)
        stat = jnp.zeros((tok, HD), F32)
        for g in range(group):
            q = qbuf[src, g * tok : (g + 1) * tok, :]
            sc = jnp.dot(q, kt[:, 0:c_all], preferred_element_type=F32) * scale + cache_bias
            sn = jnp.dot(q, kt[:, c_all:rows], preferred_element_type=F32) * scale + new_bias
            top = jnp.maximum(
                jnp.max(sc, axis=1, keepdims=True), jnp.max(sn, axis=1, keepdims=True)
            )
            pc = jnp.exp2(sc - top).astype(BF16)
            pn = jnp.exp2(sn - top).astype(BF16)
            o = jnp.dot(pc, vext[0:c_all, :], preferred_element_type=F32) + jnp.dot(
                pn, vext[c_all:rows, :], preferred_element_type=F32
            )
            total = o[:, HD : 2 * HD]
            osend[s, g * tok : (g + 1) * tok, :] = (o[:, 0:HD] / total).astype(BF16)
            stat = jnp.where(lane == g, top + jnp.log2(total), stat)
        ssend[s] = stat.T[0:8, :]

        @pl.when(s > 0)
        def _():
            for copy in o_copy(s, src):
                copy.start()

        return 0

    lax.fori_loop(0, n_chip, step, 0)
    orecv[chip] = osend[0]
    srecv[chip] = ssend[0]

    def o_wait(s, _):
        src = (chip + s) % n_chip
        remote(
            osend.at[s], orecv.at[src], o_send.at[s], o_recv.at[src], {"ctx": src * 2 + core}
        ).wait_recv()
        remote(
            ssend.at[s], srecv.at[src], s_send.at[s], s_recv.at[src], {"ctx": src * 2 + core}
        ).wait_recv()
        return 0

    lax.fori_loop(1, n_chip, o_wait, 0)

    stats = srecv[...]
    peak = jnp.max(stats, axis=0, keepdims=True)
    share = jnp.exp2(stats - peak)
    share = share / jnp.sum(share, axis=0, keepdims=True)
    share = share.reshape(n_chip * 8, tok)
    if n_chip * 8 < HD:
        share = jnp.concatenate([share, jnp.zeros((HD - n_chip * 8, tok), F32)], axis=0)
    share = share.T
    for g in range(group):
        value = jnp.zeros((tok, HD), F32)
        for i in range(n_chip):
            part = orecv[i, g * tok : (g + 1) * tok, :].astype(F32)
            value = value + share[:, i * 8 + g : i * 8 + g + 1] * part
        att[:, g * HD : (g + 1) * HD] = value.astype(BF16)

    ow_copy.wait()
    half = width // 2
    tile = min(512, half)

    def p_copy(h, s):
        peer = (ex + s) % n_exp
        columns = pl.ds(h * half, half)
        return remote(
            psend.at[pl.ds(pl.multiple_of(peer * sub, sub), sub), columns],
            precv.at[ex, :, columns],
            p_send.at[h, s],
            p_recv.at[h, ex],
            {"exp": peer},
        )

    for h in range(2):

        def project(n, _, h=h):
            columns = pl.ds(pl.multiple_of(h * half + n * tile, tile), tile)
            psend[:, columns] = jnp.dot(
                att[...], ow_v[:, columns], preferred_element_type=F32
            ).astype(BF16)
            return 0

        lax.fori_loop(0, half // tile, project, 0)

        def p_start(s, _, h=h):
            p_copy(h, s).start()
            return 0

        lax.fori_loop(1, n_exp, p_start, 0)

    precv[ex] = psend[pl.ds(pl.multiple_of(ex * sub, sub), sub), :]
    for h in range(2):
        columns = pl.ds(h * half, half)

        def p_wait(s, _, h=h, columns=columns):
            src = (ex + s) % n_exp
            remote(
                psend.at[pl.ds(0, sub), columns],
                precv.at[src, :, columns],
                p_send.at[h, s],
                p_recv.at[h, src],
                {"exp": src},
            ).wait_recv()
            return 0

        lax.fori_loop(1, n_exp, p_wait, 0)
        value = res_ref[:, columns].astype(F32)
        for j in range(n_exp):
            value = value + precv[j, :, columns].astype(F32)
        mixed_ref[:, columns] = value

    mixed = mixed_ref[...]
    square = jnp.mean(mixed * mixed, axis=1, keepdims=True)
    own = pl.ds(pl.multiple_of(ex * sub, sub), sub)
    nbuf[own, :] = (mixed * lax.rsqrt(square + EPS) * gain_ref[...].astype(F32)).astype(BF16)

    def n_copy(s, row_of, peer):
        at = pl.ds(pl.multiple_of(row_of * sub, sub), sub)
        return remote(nbuf.at[at], nbuf.at[at], n_send.at[s], n_recv.at[row_of], {"exp": peer})

    def n_start(s, _):
        n_copy(s, ex, (ex + s) % n_exp).start()
        return 0

    lax.fori_loop(1, n_exp, n_start, 0)

    def n_wait(s, _):
        src = (ex + s) % n_exp
        n_copy(s, src, src).wait_recv()
        return 0

    lax.fori_loop(1, n_exp, n_wait, 0)
    out_ref[...] = jnp.dot(sel_ref[...], nbuf[...], preferred_element_type=F32).astype(BF16)

    for copy in kv_copies:
        copy.wait_send()

    def drain_chip(s, _):
        q_copy(s).wait_send()
        for copy in o_copy(s, (chip + s) % n_chip):
            copy.wait_send()
        return 0

    def drain_exp(s, _):
        n_copy(s, ex, (ex + s) % n_exp).wait_send()
        for h in range(2):
            p_copy(h, s).wait_send()
        return 0

    lax.fori_loop(1, n_chip, drain_chip, 0)
    lax.fori_loop(1, n_exp, drain_exp, 0)


def attend(limit, q, nk, nv, ck, cv, res, ow, gain, sel):
    n_ctx, n_exp = lax.axis_size("ctx"), lax.axis_size("exp")
    n_chip = n_ctx // 2
    tok, q_width = q.shape
    cache = ck.shape[0]
    sub, width = res.shape
    rows = 2 * (cache + tok)
    block = (q_width // HD) * tok
    vmem = pl.BlockSpec(memory_space=pltpu.VMEM)
    dma = pltpu.SemaphoreType.DMA
    flops = 4 * n_chip * block * rows * HD + 2 * tok * q_width * width
    return pl.pallas_call(
        functools.partial(attend_kernel, n_ctx, n_exp),
        out_shape=(
            jax.ShapeDtypeStruct((sel.shape[0], width), BF16),
            jax.ShapeDtypeStruct((sub, width), F32),
        ),
        in_specs=[pl.BlockSpec(memory_space=pltpu.SMEM)]
        + [vmem] * 6
        + [pl.BlockSpec(memory_space=pl.ANY)]
        + [vmem] * 2,
        out_specs=(vmem, vmem),
        scratch_shapes=[
            pltpu.VMEM((rows, HD), BF16),
            pltpu.VMEM((rows, HD), BF16),
            pltpu.VMEM((HD, rows), BF16),
            pltpu.VMEM((rows, 2 * HD), BF16),
            pltpu.VMEM((n_chip, block, HD), BF16),
            pltpu.VMEM((n_chip, block, HD), BF16),
            pltpu.VMEM((n_chip, block, HD), BF16),
            pltpu.VMEM((n_chip, 8, tok), F32),
            pltpu.VMEM((n_chip, 8, tok), F32),
            pltpu.VMEM((tok, q_width), BF16),
            pltpu.VMEM((q_width, width), BF16),
            pltpu.VMEM((tok, width), BF16),
            pltpu.VMEM((n_exp, sub, width), BF16),
            pltpu.VMEM((tok, width), BF16),
            dma((4,)),
            dma((4,)),
            dma((n_chip,)),
            dma((n_chip,)),
            dma((n_chip,)),
            dma((n_chip,)),
            dma((n_chip,)),
            dma((n_chip,)),
            dma((2, n_exp)),
            dma((2, n_exp)),
            dma((n_exp,)),
            dma((n_exp,)),
            dma,
        ],
        compiler_params=pltpu.CompilerParams(
            collective_id=0, has_side_effects=True, vmem_limit_bytes=48 * 2**20
        ),
        cost_estimate=pl.CostEstimate(
            flops=flops, bytes_accessed=8 * 2**20, transcendentals=n_chip * block * rows
        ),
    )(limit, q, nk, nv, ck, cv, res, ow, gain, sel)


def local(
    queries,
    new_keys,
    new_values,
    cache_keys,
    cache_values,
    cache_length,
    residual,
    out_weight,
    norm_gain,
    route_ids,
    route_gates,
    w_gate,
    w_up,
    w_down,
):
    tok_rows = queries.shape[0]
    exp_index = lax.axis_index("exp")
    capacity = 3 * tok_rows // lax.axis_size("exp")
    hits = route_ids == exp_index
    row_hit = jnp.any(hits, 1)
    order = jnp.arange(tok_rows, dtype=jnp.int32)
    earlier = row_hit[None, :] & (order[None, :] <= order[:, None])
    slot = jnp.sum(earlier.astype(jnp.int32), 1) - 1
    select = (
        (slot[None, :] == jnp.arange(capacity, dtype=jnp.int32)[:, None]) & row_hit[None, :]
    ).astype(BF16)
    outgoing, own_mixed = attend(
        cache_length,
        queries,
        new_keys,
        new_values,
        cache_keys,
        cache_values,
        residual,
        out_weight,
        norm_gain[None, :],
        select,
    )
    piece = lax.all_gather(outgoing, "ctx", axis=0, tiled=True)
    gate_part = jnp.dot(piece, w_gate[0], preferred_element_type=F32)
    up_part = jnp.dot(piece, w_up[0], preferred_element_type=F32)
    hidden = (jax.nn.silu(gate_part) * up_part).astype(BF16)
    terms = jnp.dot(hidden, w_down[0], preferred_element_type=F32)
    expert_out = lax.psum_scatter(terms.astype(BF16), "ctx", scatter_dimension=0, tiled=True)
    returned = jnp.dot(jnp.transpose(select), expert_out, preferred_element_type=F32)
    weight_row = jnp.sum(jnp.where(hits, route_gates, 0.0), 1)
    weighted = weight_row[:, None] * returned
    combined = lax.psum_scatter(
        weighted.astype(BF16), "exp", scatter_dimension=0, tiled=True
    ).astype(F32)
    return (own_mixed + combined).astype(BF16)


def solution(mesh):
    placed = (
        P("ctx", "exp"),
        P("ctx", "exp"),
        P("ctx", "exp"),
        P("ctx", "exp"),
        P("ctx", "exp"),
        P(),
        P(("ctx", "exp"), None),
        P("exp", None),
        P(),
        P("ctx", None),
        P("ctx", None),
        P("exp", None, "ctx"),
        P("exp", None, "ctx"),
        P("exp", "ctx", None),
    )
    return jax.shard_map(
        local, mesh=mesh, in_specs=placed, out_specs=P(("ctx", "exp"), None), check_vma=False
    )
```

```python
import functools
import math

import jax
import jax.numpy as jnp
from jax import lax
from jax.experimental import pallas as pl
from jax.experimental.pallas import tpu as pltpu
from jax.sharding import PartitionSpec as P

HD = 128
NEG = -1e30
EPS = 1e-05
MESH = pl.DeviceIdType.MESH
F32 = jnp.float32
BF16 = jnp.bfloat16


def remote(src, dst, send, recv, where):
    return pltpu.make_async_remote_copy(
        src_ref=src,
        dst_ref=dst,
        send_sem=send,
        recv_sem=recv,
        device_id=where,
        device_id_type=MESH,
    )


def attend_kernel(
    n_ctx,
    n_exp,
    limit_ref,
    q_ref,
    nk_ref,
    nv_ref,
    ck_ref,
    cv_ref,
    res_ref,
    ow_ref,
    gain_ref,
    sel_ref,
    out_ref,
    mixed_ref,
    kbuf,
    vbuf,
    kt,
    vext,
    qbuf,
    osend,
    orecv,
    ssend,
    srecv,
    att,
    ow_v,
    psend,
    precv,
    nbuf,
    kv_send,
    kv_recv,
    q_send,
    q_recv,
    o_send,
    o_recv,
    s_send,
    s_recv,
    p_send,
    p_recv,
    n_send,
    n_recv,
    ow_sem,
):
    n_chip = n_ctx // 2
    me = lax.axis_index("ctx")
    ex = lax.axis_index("exp")
    chip = me // 2
    core = me % 2
    sib = me + 1 - 2 * core
    tok = q_ref.shape[0]
    group = q_ref.shape[1] // HD
    cache = ck_ref.shape[0]
    width = res_ref.shape[1]
    sub = res_ref.shape[0]
    c_all = 2 * cache
    rows = c_all + 2 * tok

    ow_copy = pltpu.make_async_copy(ow_ref, ow_v, ow_sem)
    ow_copy.start()

    barrier = pltpu.get_barrier_semaphore()

    def greet_chip(s, _):
        peer = ((chip + s) % n_chip) * 2 + core
        pl.semaphore_signal(barrier, inc=1, device_id={"ctx": peer}, device_id_type=MESH)
        return 0

    def greet_exp(s, _):
        pl.semaphore_signal(
            barrier, inc=1, device_id={"exp": (ex + s) % n_exp}, device_id_type=MESH
        )
        return 0

    pl.semaphore_signal(barrier, inc=1, device_id={"ctx": sib}, device_id_type=MESH)
    lax.fori_loop(1, n_chip, greet_chip, 0)
    lax.fori_loop(1, n_exp, greet_exp, 0)

    for g in range(group):
        qbuf[chip, g * tok : (g + 1) * tok, :] = q_ref[:, g * HD : (g + 1) * HD]
    kbuf[0:cache, :] = ck_ref[...]
    kbuf[c_all : c_all + tok, :] = nk_ref[...]
    vbuf[0:cache, :] = cv_ref[...]
    vbuf[c_all : c_all + tok, :] = nv_ref[...]

    pl.semaphore_wait(barrier, n_chip + n_exp - 1)

    kv_copies = [
        remote(src, dst, kv_send.at[i], kv_recv.at[i], {"ctx": sib})
        for i, (src, dst) in enumerate(
            [
                (ck_ref, kbuf.at[pl.ds(cache, cache)]),
                (nk_ref, kbuf.at[pl.ds(c_all + tok, tok)]),
                (cv_ref, vbuf.at[pl.ds(cache, cache)]),
                (nv_ref, vbuf.at[pl.ds(c_all + tok, tok)]),
            ]
        )
    ]
    for copy in kv_copies:
        copy.start()

    def q_copy(s):
        peer = ((chip + n_chip - s) % n_chip) * 2 + core
        return remote(
            qbuf.at[chip], qbuf.at[chip], q_send.at[s], q_recv.at[chip], {"ctx": peer}
        )

    def q_start(s, _):
        q_copy(s).start()
        return 0

    lax.fori_loop(1, n_chip, q_start, 0)

    for copy in kv_copies:
        copy.wait_recv()
    kt[...] = kbuf[...].T
    vext[:, 0:HD] = vbuf[...]
    vext[:, HD : 2 * HD] = jnp.ones((rows, HD), BF16)

    limit = limit_ref[0]
    position = lax.broadcasted_iota(jnp.int32, (1, cache), 1)
    bias_own = jnp.where(position + me * cache < limit, 0.0, NEG)
    bias_sib = jnp.where(position + sib * cache < limit, 0.0, NEG)
    cache_bias = jnp.concatenate([bias_own, bias_sib], axis=1)
    t_row = lax.broadcasted_iota(jnp.int32, (tok, 2 * tok), 0)
    t_col = lax.broadcasted_iota(jnp.int32, (tok, 2 * tok), 1)
    lane = lax.broadcasted_iota(jnp.int32, (tok, HD), 1)
    key_at = jnp.where(t_col < tok, t_col + me * tok, t_col - tok + sib * tok)
    scale = math.log2(math.e) / math.sqrt(HD)

    def o_copy(s, src):
        peer = src * 2 + core
        return (
            remote(osend.at[s], orecv.at[chip], o_send.at[s], o_recv.at[chip], {"ctx": peer}),
            remote(ssend.at[s], srecv.at[chip], s_send.at[s], s_recv.at[chip], {"ctx": peer}),
        )

    def step(s, _):
        src = (chip + s) % n_chip

        @pl.when(s > 0)
        def _():
            remote(
                qbuf.at[src], qbuf.at[src], q_send.at[s], q_recv.at[src], {"ctx": src * 2 + core}
            ).wait_recv()

        query_at = t_row + (src * 2 + core) * tok
        new_bias = jnp.where(key_at <= query_at, 0.0, NEG)
        stat = jnp.zeros((tok, HD), F32)
        for g in range(group):
            q = qbuf[src, g * tok : (g + 1) * tok, :]
            sc = jnp.dot(q, kt[:, 0:c_all], preferred_element_type=F32) * scale + cache_bias
            sn = jnp.dot(q, kt[:, c_all:rows], preferred_element_type=F32) * scale + new_bias
            top = jnp.maximum(
                jnp.max(sc, axis=1, keepdims=True), jnp.max(sn, axis=1, keepdims=True)
            )
            pc = jnp.exp2(sc - top).astype(BF16)
            pn = jnp.exp2(sn - top).astype(BF16)
            o = jnp.dot(pc, vext[0:c_all, :], preferred_element_type=F32) + jnp.dot(
                pn, vext[c_all:rows, :], preferred_element_type=F32
            )
            total = o[:, HD : 2 * HD]
            osend[s, g * tok : (g + 1) * tok, :] = (o[:, 0:HD] / total).astype(BF16)
            stat = jnp.where(lane == g, top + jnp.log2(total), stat)
        ssend[s] = stat.T[0:8, :]

        @pl.when(s > 0)
        def _():
            for copy in o_copy(s, src):
                copy.start()

        return 0

    lax.fori_loop(0, n_chip, step, 0)
    orecv[chip] = osend[0]
    srecv[chip] = ssend[0]

    def o_wait(s, _):
        src = (chip + s) % n_chip
        remote(
            osend.at[s], orecv.at[src], o_send.at[s], o_recv.at[src], {"ctx": src * 2 + core}
        ).wait_recv()
        remote(
            ssend.at[s], srecv.at[src], s_send.at[s], s_recv.at[src], {"ctx": src * 2 + core}
        ).wait_recv()
        return 0

    lax.fori_loop(1, n_chip, o_wait, 0)

    stats = srecv[...]
    peak = jnp.max(stats, axis=0, keepdims=True)
    share = jnp.exp2(stats - peak)
    share = share / jnp.sum(share, axis=0, keepdims=True)
    share = share.reshape(n_chip * 8, tok)
    if n_chip * 8 < HD:
        share = jnp.concatenate([share, jnp.zeros((HD - n_chip * 8, tok), F32)], axis=0)
    share = share.T
    for g in range(group):
        value = jnp.zeros((tok, HD), F32)
        for i in range(n_chip):
            part = orecv[i, g * tok : (g + 1) * tok, :].astype(F32)
            value = value + share[:, i * 8 + g : i * 8 + g + 1] * part
        att[:, g * HD : (g + 1) * HD] = value.astype(BF16)

    ow_copy.wait()
    half = width // 2
    tile = min(512, half)

    def p_copy(h, s):
        peer = (ex + s) % n_exp
        columns = pl.ds(h * half, half)
        return remote(
            psend.at[pl.ds(pl.multiple_of(peer * sub, sub), sub), columns],
            precv.at[ex, :, columns],
            p_send.at[h, s],
            p_recv.at[h, ex],
            {"exp": peer},
        )

    for h in range(2):

        def project(n, _, h=h):
            columns = pl.ds(pl.multiple_of(h * half + n * tile, tile), tile)
            psend[:, columns] = jnp.dot(
                att[...], ow_v[:, columns], preferred_element_type=F32
            ).astype(BF16)
            return 0

        lax.fori_loop(0, half // tile, project, 0)

        def p_start(s, _, h=h):
            p_copy(h, s).start()
            return 0

        lax.fori_loop(1, n_exp, p_start, 0)

    precv[ex] = psend[pl.ds(pl.multiple_of(ex * sub, sub), sub), :]
    for h in range(2):
        columns = pl.ds(h * half, half)

        def p_wait(s, _, h=h, columns=columns):
            src = (ex + s) % n_exp
            remote(
                psend.at[pl.ds(0, sub), columns],
                precv.at[src, :, columns],
                p_send.at[h, s],
                p_recv.at[h, src],
                {"exp": src},
            ).wait_recv()
            return 0

        lax.fori_loop(1, n_exp, p_wait, 0)
        value = res_ref[:, columns].astype(F32)
        for j in range(n_exp):
            value = value + precv[j, :, columns].astype(F32)
        mixed_ref[:, columns] = value

    mixed = mixed_ref[...]
    square = jnp.mean(mixed * mixed, axis=1, keepdims=True)
    own = pl.ds(pl.multiple_of(ex * sub, sub), sub)
    nbuf[own, :] = (mixed * lax.rsqrt(square + EPS) * gain_ref[...].astype(F32)).astype(BF16)

    def n_copy(s, row_of, peer):
        at = pl.ds(pl.multiple_of(row_of * sub, sub), sub)
        return remote(nbuf.at[at], nbuf.at[at], n_send.at[s], n_recv.at[row_of], {"exp": peer})

    def n_start(s, _):
        n_copy(s, ex, (ex + s) % n_exp).start()
        return 0

    lax.fori_loop(1, n_exp, n_start, 0)

    def n_wait(s, _):
        src = (ex + s) % n_exp
        n_copy(s, src, src).wait_recv()
        return 0

    lax.fori_loop(1, n_exp, n_wait, 0)
    out_ref[...] = jnp.dot(sel_ref[...], nbuf[...], preferred_element_type=F32).astype(BF16)

    for copy in kv_copies:
        copy.wait_send()

    def drain_chip(s, _):
        q_copy(s).wait_send()
        for copy in o_copy(s, (chip + s) % n_chip):
            copy.wait_send()
        return 0

    def drain_exp(s, _):
        n_copy(s, ex, (ex + s) % n_exp).wait_send()
        for h in range(2):
            p_copy(h, s).wait_send()
        return 0

    lax.fori_loop(1, n_chip, drain_chip, 0)
    lax.fori_loop(1, n_exp, drain_exp, 0)


def attend(limit, q, nk, nv, ck, cv, res, ow, gain, sel):
    n_ctx, n_exp = lax.axis_size("ctx"), lax.axis_size("exp")
    n_chip = n_ctx // 2
    tok, q_width = q.shape
    cache = ck.shape[0]
    sub, width = res.shape
    rows = 2 * (cache + tok)
    block = (q_width // HD) * tok
    vmem = pl.BlockSpec(memory_space=pltpu.VMEM)
    dma = pltpu.SemaphoreType.DMA
    flops = 4 * n_chip * block * rows * HD + 2 * tok * q_width * width
    return pl.pallas_call(
        functools.partial(attend_kernel, n_ctx, n_exp),
        out_shape=(
            jax.ShapeDtypeStruct((sel.shape[0], width), BF16),
            jax.ShapeDtypeStruct((sub, width), F32),
        ),
        in_specs=[pl.BlockSpec(memory_space=pltpu.SMEM)]
        + [vmem] * 6
        + [pl.BlockSpec(memory_space=pl.ANY)]
        + [vmem] * 2,
        out_specs=(vmem, vmem),
        scratch_shapes=[
            pltpu.VMEM((rows, HD), BF16),
            pltpu.VMEM((rows, HD), BF16),
            pltpu.VMEM((HD, rows), BF16),
            pltpu.VMEM((rows, 2 * HD), BF16),
            pltpu.VMEM((n_chip, block, HD), BF16),
            pltpu.VMEM((n_chip, block, HD), BF16),
            pltpu.VMEM((n_chip, block, HD), BF16),
            pltpu.VMEM((n_chip, 8, tok), F32),
            pltpu.VMEM((n_chip, 8, tok), F32),
            pltpu.VMEM((tok, q_width), BF16),
            pltpu.VMEM((q_width, width), BF16),
            pltpu.VMEM((tok, width), BF16),
            pltpu.VMEM((n_exp, sub, width), BF16),
            pltpu.VMEM((tok, width), BF16),
            dma((4,)),
            dma((4,)),
            dma((n_chip,)),
            dma((n_chip,)),
            dma((n_chip,)),
            dma((n_chip,)),
            dma((n_chip,)),
            dma((n_chip,)),
            dma((2, n_exp)),
            dma((2, n_exp)),
            dma((n_exp,)),
            dma((n_exp,)),
            dma,
        ],
        compiler_params=pltpu.CompilerParams(
            collective_id=0, has_side_effects=True, vmem_limit_bytes=48 * 2**20
        ),
        cost_estimate=pl.CostEstimate(
            flops=flops, bytes_accessed=8 * 2**20, transcendentals=n_chip * block * rows
        ),
    )(limit, q, nk, nv, ck, cv, res, ow, gain, sel)


def expert_kernel(
    n_ctx,
    n_exp,
    chunks,
    in_ref,
    wg_ref,
    wu_ref,
    wd_ref,
    back_ref,
    gate_ref,
    mixed_ref,
    out_ref,
    xall,
    wg_v,
    wu_v,
    wd_v,
    acc_g,
    acc_u,
    hid,
    tbuf,
    sbuf,
    red,
    hbuf,
    pbuf,
    xbuf,
    wsend,
    wrecv,
    wg_sem,
    wu_sem,
    wd_sem,
    a_send,
    a_recv,
    r_send,
    r_recv,
    e_send,
    e_recv,
):
    n_y = n_ctx // 4
    me = lax.axis_index("ctx")
    ex = lax.axis_index("exp")
    core = me % 2
    x = me // (2 * n_y)
    y = (me // 2) % n_y
    y_up, y_down, y_far = (y + 1) % n_y, (y + n_y - 1) % n_y, (y + 2) % n_y
    sib = {"ctx": me + 1 - 2 * core}
    across = {"ctx": ((1 - x) * n_y + y) * 2 + core}
    up = {"ctx": (x * n_y + y_up) * 2 + core}
    down = {"ctx": (x * n_y + y_down) * 2 + core}
    cap, width = in_ref.shape
    sub = out_ref.shape[0]
    pair = 2 * cap
    side = n_y * pair
    span = width // chunks

    def cols(c):
        return pl.ds(pl.multiple_of(c * span, span), span)

    def w_copies(c):
        at = pl.ds(pl.multiple_of(c * span, span), span)
        return (
            pltpu.make_async_copy(wg_ref.at[at], wg_v.at[at], wg_sem.at[c]),
            pltpu.make_async_copy(wu_ref.at[at], wu_v.at[at], wu_sem.at[c]),
        )

    def w_start(c, _):
        for copy in w_copies(c):
            copy.start()
        return 0

    lax.fori_loop(0, chunks, w_start, 0)
    wd_copy = pltpu.make_async_copy(wd_ref, wd_v, wd_sem)
    wd_copy.start()

    barrier = pltpu.get_barrier_semaphore()
    for where in (sib, across, up, down):
        pl.semaphore_signal(barrier, inc=1, device_id=where, device_id_type=MESH)

    def greet_exp(s, _):
        pl.semaphore_signal(
            barrier, inc=1, device_id={"exp": (ex + s) % n_exp}, device_id_type=MESH
        )
        return 0

    lax.fori_loop(1, n_exp, greet_exp, 0)

    def row(k, at, offset=0):
        return pl.multiple_of(k * side + at * pair + offset, 16)

    own_row = row(core, y, x * cap)
    xall[pl.ds(own_row, cap), :] = in_ref[...]
    acc_g[...] = jnp.zeros_like(acc_g)
    acc_u[...] = jnp.zeros_like(acc_u)
    pl.semaphore_wait(barrier, 3 + n_exp)

    def gather(kind, c, first, count, where):
        ref = xall.at[pl.ds(first, count), cols(c)]
        return remote(ref, ref, a_send.at[kind, c], a_recv.at[kind, c], where)

    def a_x(c):
        return gather(0, c, own_row, cap, across)

    def a_pairs(c):
        return (
            gather(1, c, row(core, y), pair, up),
            gather(2, c, row(core, y), pair, down),
            gather(5, c, row(core, y), pair, sib),
        )

    def a_relays(c):
        return (
            gather(3, c, row(core, y_down), cap, up),
            gather(4, c, row(core, y_up, cap), cap, down),
            gather(6, c, row(core, y_down), pair, sib),
            gather(7, c, row(core, y_up), pair, sib),
        )

    def a_far(c):
        return gather(8, c, row(core, y_far), pair, sib)

    def a_x_start(c, _):
        a_x(c).start()
        return 0

    lax.fori_loop(0, chunks, a_x_start, 0)

    def gather_step(it, _):
        @pl.when(it < chunks)
        def _():
            c = it
            gather(0, c, row(core, y, (1 - x) * cap), cap, across).wait_recv()
            for copy in a_pairs(c):
                copy.start()

        @pl.when((it >= 1) & (it < chunks + 1))
        def _():
            c = it - 1
            gather(1, c, row(core, y_down), pair, down).wait_recv()
            gather(2, c, row(core, y_up), pair, up).wait_recv()
            for copy in a_relays(c):
                copy.start()

        @pl.when((it >= 2) & (it < chunks + 2))
        def _():
            c = it - 2
            gather(3, c, row(core, y_far), cap, down).wait_recv()
            gather(4, c, row(core, y_far, cap), cap, up).wait_recv()
            a_far(c).start()

        @pl.when(it >= 3)
        def _():
            c = it - 3
            gather(5, c, row(1 - core, y), pair, sib).wait_recv()
            gather(6, c, row(1 - core, y_down), pair, sib).wait_recv()
            gather(7, c, row(1 - core, y_up), pair, sib).wait_recv()
            gather(8, c, row(1 - core, y_far), pair, sib).wait_recv()
            for copy in w_copies(c):
                copy.wait()
            lhs = xall[:, cols(c)]
            acc_g[...] += jnp.dot(lhs, wg_v[cols(c), :], preferred_element_type=F32)
            acc_u[...] += jnp.dot(lhs, wu_v[cols(c), :], preferred_element_type=F32)

        return 0

    lax.fori_loop(0, chunks + 3, gather_step, 0)

    gate = acc_g[...]
    hid[...] = (gate / (1.0 + jnp.exp(-gate)) * acc_u[...]).astype(BF16)
    wd_copy.wait()

    def reduce(kind, c, src, dst, where):
        return remote(src, dst, r_send.at[kind, c], r_recv.at[kind, c], where)

    def r_sib(c):
        other = pl.ds(pl.multiple_of((1 - core) * side, 16), side)
        return reduce(0, c, tbuf.at[c, other], sbuf.at[c], sib)

    def block(at, offset, count):
        return pl.ds(pl.multiple_of(at * pair + offset, 16), count)

    def r_halves(c):
        return (
            reduce(1, c, red.at[c, block(y_far, 0, cap)], hbuf.at[0, c], up),
            reduce(2, c, red.at[c, block(y_far, cap, cap)], hbuf.at[1, c], down),
        )

    def r_pairs(c):
        return (
            reduce(3, c, red.at[c, block(y_up, 0, pair)], pbuf.at[0, c], up),
            reduce(4, c, red.at[c, block(y_down, 0, pair)], pbuf.at[1, c], down),
        )

    def r_x(c):
        return reduce(5, c, red.at[c, block(y, (1 - x) * cap, cap)], xbuf.at[c], across)

    def e_copy(c, s, row_of, slot, peer):
        at = pl.ds(pl.multiple_of(row_of * sub, sub), sub)
        return remote(
            wsend.at[at, cols(c)],
            wrecv.at[slot, :, cols(c)],
            e_send.at[s, c],
            e_recv.at[slot, c],
            {"exp": peer},
        )

    def add(c, at, other):
        red[c, at, :] = (red[c, at, :].astype(F32) + other.astype(F32)).astype(BF16)

    def reduce_step(it, _):
        @pl.when(it >= 5)
        def _():
            c = it - 5

            def wait(s, _):
                src = (ex + s) % n_exp
                e_copy(c, s, src, src, src).wait_recv()
                return 0

            lax.fori_loop(1, n_exp, wait, 0)
            value = jnp.zeros((sub, span), F32)
            for j in range(n_exp):
                value = value + wrecv[j, :, cols(c)].astype(F32)
            out_ref[:, cols(c)] = (mixed_ref[:, cols(c)] + value).astype(BF16)

        @pl.when((it >= 4) & (it < chunks + 4))
        def _():
            c = it - 4
            r_x(c).wait_recv()
            own = block(y, x * cap, cap)
            done = (red[c, own, :].astype(F32) + xbuf[c].astype(F32)).astype(BF16)
            back = jnp.dot(back_ref[...], done, preferred_element_type=F32)
            wsend[:, cols(c)] = (gate_ref[...] * back).astype(BF16)

            def start(s, _):
                peer = (ex + s) % n_exp
                e_copy(c, s, peer, ex, peer).start()
                return 0

            lax.fori_loop(1, n_exp, start, 0)
            own_rows = pl.ds(pl.multiple_of(ex * sub, sub), sub)
            wrecv[ex, :, cols(c)] = wsend[own_rows, cols(c)]

        @pl.when((it >= 3) & (it < chunks + 3))
        def _():
            c = it - 3
            for copy in r_pairs(c):
                copy.wait_recv()
            add(c, block(y, 0, pair), pbuf[0, c].astype(F32) + pbuf[1, c].astype(F32))
            r_x(c).start()

        @pl.when((it >= 2) & (it < chunks + 2))
        def _():
            c = it - 2
            for copy in r_halves(c):
                copy.wait_recv()
            add(c, block(y_up, 0, cap), hbuf[0, c])
            add(c, block(y_down, cap, cap), hbuf[1, c])
            for copy in r_pairs(c):
                copy.start()

        @pl.when((it >= 1) & (it < chunks + 1))
        def _():
            c = it - 1
            r_sib(c).wait_recv()
            own = pl.ds(pl.multiple_of(core * side, 16), side)
            red[c] = (tbuf[c, own, :].astype(F32) + sbuf[c].astype(F32)).astype(BF16)
            for copy in r_halves(c):
                copy.start()

        @pl.when(it < chunks)
        def _():
            c = it
            tbuf[c] = jnp.dot(hid[...], wd_v[:, cols(c)], preferred_element_type=F32).astype(BF16)
            r_sib(c).start()

        return 0

    lax.fori_loop(0, chunks + 5, reduce_step, 0)

    def drain(c, _):
        for copy in (a_x(c), *a_pairs(c), *a_relays(c), a_far(c)):
            copy.wait_send()
        for copy in (r_sib(c), *r_halves(c), *r_pairs(c), r_x(c)):
            copy.wait_send()

        def drain_exp(s, _):
            peer = (ex + s) % n_exp
            e_copy(c, s, peer, ex, peer).wait_send()
            return 0

        lax.fori_loop(1, n_exp, drain_exp, 0)
        return 0

    lax.fori_loop(0, chunks, drain, 0)


def experts(rows_in, wg, wu, wd, back, gate, mixed):
    n_ctx, n_exp = lax.axis_size("ctx"), lax.axis_size("exp")
    cap, width = rows_in.shape
    hidden = wg.shape[1]
    tok = back.shape[0]
    sub = mixed.shape[0]
    chunks = 8
    span = width // chunks
    total = n_ctx * cap
    side = total // 2
    vmem = pl.BlockSpec(memory_space=pltpu.VMEM)
    hbm = pl.BlockSpec(memory_space=pl.ANY)
    dma = pltpu.SemaphoreType.DMA
    return pl.pallas_call(
        functools.partial(expert_kernel, n_ctx, n_exp, chunks),
        out_shape=jax.ShapeDtypeStruct((sub, width), BF16),
        in_specs=[vmem, hbm, hbm, hbm, vmem, vmem, vmem],
        out_specs=vmem,
        scratch_shapes=[
            pltpu.VMEM((total, width), BF16),
            pltpu.VMEM((width, hidden), BF16),
            pltpu.VMEM((width, hidden), BF16),
            pltpu.VMEM((hidden, width), BF16),
            pltpu.VMEM((total, hidden), F32),
            pltpu.VMEM((total, hidden), F32),
            pltpu.VMEM((total, hidden), BF16),
            pltpu.VMEM((chunks, total, span), BF16),
            pltpu.VMEM((chunks, side, span), BF16),
            pltpu.VMEM((chunks, side, span), BF16),
            pltpu.VMEM((2, chunks, cap, span), BF16),
            pltpu.VMEM((2, chunks, 2 * cap, span), BF16),
            pltpu.VMEM((chunks, cap, span), BF16),
            pltpu.VMEM((tok, width), BF16),
            pltpu.VMEM((n_exp, sub, width), BF16),
            dma((chunks,)),
            dma((chunks,)),
            dma,
            dma((9, chunks)),
            dma((9, chunks)),
            dma((6, chunks)),
            dma((6, chunks)),
            dma((n_exp, chunks)),
            dma((n_exp, chunks)),
        ],
        compiler_params=pltpu.CompilerParams(
            collective_id=1, has_side_effects=True, vmem_limit_bytes=60 * 2**20
        ),
        cost_estimate=pl.CostEstimate(
            flops=6 * total * width * hidden,
            bytes_accessed=6 * width * hidden,
            transcendentals=total * hidden,
        ),
    )(rows_in, wg, wu, wd, back, gate, mixed)


def local(
    queries,
    new_keys,
    new_values,
    cache_keys,
    cache_values,
    cache_length,
    residual,
    out_weight,
    norm_gain,
    route_ids,
    route_gates,
    w_gate,
    w_up,
    w_down,
):
    tok_rows = queries.shape[0]
    exp_index = lax.axis_index("exp")
    capacity = 3 * tok_rows // lax.axis_size("exp")
    hits = route_ids == exp_index
    row_hit = jnp.any(hits, 1)
    order = jnp.arange(tok_rows, dtype=jnp.int32)
    earlier = row_hit[None, :] & (order[None, :] <= order[:, None])
    slot = jnp.sum(earlier.astype(jnp.int32), 1) - 1
    select = (
        (slot[None, :] == jnp.arange(capacity, dtype=jnp.int32)[:, None]) & row_hit[None, :]
    ).astype(BF16)
    outgoing, own_mixed = attend(
        cache_length,
        queries,
        new_keys,
        new_values,
        cache_keys,
        cache_values,
        residual,
        out_weight,
        norm_gain[None, :],
        select,
    )
    weight_row = jnp.sum(jnp.where(hits, route_gates, 0.0), 1)
    return experts(
        outgoing,
        w_gate[0],
        w_up[0],
        w_down[0],
        jnp.transpose(select),
        weight_row[:, None],
        own_mixed,
    )


def solution(mesh):
    placed = (
        P("ctx", "exp"),
        P("ctx", "exp"),
        P("ctx", "exp"),
        P("ctx", "exp"),
        P("ctx", "exp"),
        P(),
        P(("ctx", "exp"), None),
        P("exp", None),
        P(),
        P("ctx", None),
        P("ctx", None),
        P("exp", None, "ctx"),
        P("exp", None, "ctx"),
        P("exp", "ctx", None),
    )
    return jax.shard_map(
        local, mesh=mesh, in_specs=placed, out_specs=P(("ctx", "exp"), None), check_vma=False
    )
```

```python
import functools
import math

import jax
import jax.numpy as jnp
from jax import lax
from jax.experimental import pallas as pl
from jax.experimental.pallas import tpu as pltpu
from jax.sharding import PartitionSpec as P

HD = 128
NEG = -1e30
EPS = 1e-05
MESH = pl.DeviceIdType.MESH
F32 = jnp.float32
BF16 = jnp.bfloat16


def remote(src, dst, send, recv, where):
    return pltpu.make_async_remote_copy(
        src_ref=src,
        dst_ref=dst,
        send_sem=send,
        recv_sem=recv,
        device_id=where,
        device_id_type=MESH,
    )


def arrived(ref, sem):
    pltpu.make_async_copy(ref, ref, sem).wait()


def attend_kernel(
    n_ctx,
    n_exp,
    limit_ref,
    q_ref,
    nk_ref,
    nv_ref,
    ck_ref,
    cv_ref,
    res_ref,
    ow_ref,
    gain_ref,
    normed_ref,
    mixed_ref,
    kbuf,
    vbuf,
    kt,
    vext,
    qbuf,
    osend,
    orecv,
    ssend,
    srecv,
    att,
    ow_v,
    psend,
    precv,
    res_v,
    gain_v,
    in_sem,
    kv_send,
    kv_recv,
    q_send,
    q_recv,
    o_send,
    o_recv,
    s_send,
    s_recv,
    p_send,
    p_recv,
    ow_sem,
):
    n_chip = n_ctx // 2
    me = lax.axis_index("ctx")
    ex = lax.axis_index("exp")
    chip = me // 2
    core = me % 2
    sib = me + 1 - 2 * core
    tok = q_ref.shape[0]
    group = q_ref.shape[1] // HD
    cache = ck_ref.shape[0]
    sub, width = res_ref.shape
    c_all = 2 * cache
    rows = c_all + 2 * tok

    ow_copy = pltpu.make_async_copy(ow_ref, ow_v, ow_sem)
    barrier = pltpu.get_barrier_semaphore()

    def greet_chip(s, _):
        peer = ((chip + s) % n_chip) * 2 + core
        pl.semaphore_signal(barrier, inc=1, device_id={"ctx": peer}, device_id_type=MESH)
        return 0

    def greet_exp(s, _):
        pl.semaphore_signal(
            barrier, inc=1, device_id={"exp": (ex + s) % n_exp}, device_id_type=MESH
        )
        return 0

    pl.semaphore_signal(barrier, inc=1, device_id={"ctx": sib}, device_id_type=MESH)
    lax.fori_loop(1, n_chip, greet_chip, 0)
    lax.fori_loop(1, n_exp, greet_exp, 0)

    moves = [
        (q_ref.at[:, pl.ds(g * HD, HD)], qbuf.at[chip, pl.ds(g * tok, tok)]) for g in range(group)
    ]
    moves += [
        (ck_ref, kbuf.at[pl.ds(0, cache)]),
        (nk_ref, kbuf.at[pl.ds(c_all, tok)]),
        (cv_ref, vbuf.at[pl.ds(0, cache)]),
        (nv_ref, vbuf.at[pl.ds(c_all, tok)]),
        (res_ref, res_v),
        (gain_ref, gain_v),
    ]
    loads = [pltpu.make_async_copy(a, b, in_sem.at[i]) for i, (a, b) in enumerate(moves)]
    for load in loads:
        load.start()
    for load in loads[0:group]:
        load.wait()
    pl.semaphore_wait(barrier, n_chip + n_exp - 1)

    kv_copies = [
        remote(src, dst, kv_send.at[i], kv_recv.at[i], {"ctx": sib})
        for i, (src, dst) in enumerate(
            [
                (ck_ref, kbuf.at[pl.ds(cache, cache)]),
                (nk_ref, kbuf.at[pl.ds(c_all + tok, tok)]),
                (cv_ref, vbuf.at[pl.ds(cache, cache)]),
                (nv_ref, vbuf.at[pl.ds(c_all + tok, tok)]),
            ]
        )
    ]
    for copy in kv_copies:
        copy.start()

    def q_copy(s):
        peer = ((chip + n_chip - s) % n_chip) * 2 + core
        return remote(
            qbuf.at[chip], qbuf.at[chip], q_send, q_recv.at[chip], {"ctx": peer}
        )

    def q_start(s, _):
        q_copy(s).start()
        return 0

    lax.fori_loop(1, n_chip, q_start, 0)
    ow_copy.start()
    for load in loads[group:]:
        load.wait()

    for copy in kv_copies:
        copy.wait_recv()
    kt[...] = kbuf[...].T
    vext[:, 0:HD] = vbuf[...]
    vext[:, HD : 2 * HD] = jnp.ones((rows, HD), BF16)

    limit = limit_ref[0]
    position = lax.broadcasted_iota(jnp.int32, (1, cache), 1)
    bias_own = jnp.where(position + me * cache < limit, 0.0, NEG)
    bias_sib = jnp.where(position + sib * cache < limit, 0.0, NEG)
    cache_bias = jnp.concatenate([bias_own, bias_sib], axis=1)
    t_row = lax.broadcasted_iota(jnp.int32, (tok, 2 * tok), 0)
    t_col = lax.broadcasted_iota(jnp.int32, (tok, 2 * tok), 1)
    lane = lax.broadcasted_iota(jnp.int32, (tok, HD), 1)
    key_at = jnp.where(t_col < tok, t_col + me * tok, t_col - tok + sib * tok)
    scale = math.log2(math.e) / math.sqrt(HD)

    def o_copy(s, src):
        peer = src * 2 + core
        return (
            remote(osend.at[s], orecv.at[chip], o_send, o_recv, {"ctx": peer}),
            remote(ssend.at[s], srecv.at[chip], s_send, s_recv, {"ctx": peer}),
        )

    def step(s, _):
        src = (chip + s) % n_chip

        @pl.when(s > 0)
        def _():
            arrived(qbuf.at[src], q_recv.at[src])

        query_at = t_row + (src * 2 + core) * tok
        new_bias = jnp.where(key_at <= query_at, 0.0, NEG)
        stat = jnp.zeros((tok, HD), F32)
        for g in range(group):
            q = qbuf[src, g * tok : (g + 1) * tok, :]
            sc = jnp.dot(q, kt[:, 0:c_all], preferred_element_type=F32) * scale + cache_bias
            sn = jnp.dot(q, kt[:, c_all:rows], preferred_element_type=F32) * scale + new_bias
            top = jnp.maximum(
                jnp.max(sc, axis=1, keepdims=True), jnp.max(sn, axis=1, keepdims=True)
            )
            pc = jnp.exp2(sc - top).astype(BF16)
            pn = jnp.exp2(sn - top).astype(BF16)
            o = jnp.dot(pc, vext[0:c_all, :], preferred_element_type=F32) + jnp.dot(
                pn, vext[c_all:rows, :], preferred_element_type=F32
            )
            total = o[:, HD : 2 * HD]
            osend[s, g * tok : (g + 1) * tok, :] = (o[:, 0:HD] / total).astype(BF16)
            stat = jnp.where(lane == g, top + jnp.log2(total), stat)
        ssend[s] = stat.T[0:8, :]

        @pl.when(s > 0)
        def _():
            for copy in o_copy(s, src):
                copy.start()

        return 0

    lax.fori_loop(0, n_chip, step, 0)
    orecv[chip] = osend[0]
    srecv[chip] = ssend[0]

    arrived(orecv.at[pl.ds(0, n_chip - 1)], o_recv)
    arrived(srecv.at[pl.ds(0, n_chip - 1)], s_recv)

    stats = srecv[...]
    peak = jnp.max(stats, axis=0, keepdims=True)
    share = jnp.exp2(stats - peak)
    share = share / jnp.sum(share, axis=0, keepdims=True)
    share = share.reshape(n_chip * 8, tok)
    if n_chip * 8 < HD:
        share = jnp.concatenate([share, jnp.zeros((HD - n_chip * 8, tok), F32)], axis=0)
    share = share.T
    for g in range(group):
        value = jnp.zeros((tok, HD), F32)
        for i in range(n_chip):
            part = orecv[i, g * tok : (g + 1) * tok, :].astype(F32)
            value = value + share[:, i * 8 + g : i * 8 + g + 1] * part
        att[:, g * HD : (g + 1) * HD] = value.astype(BF16)

    ow_copy.wait()
    half = width // 2
    tile = min(512, half)

    def p_copy(h, s):
        peer = (ex + s) % n_exp
        columns = pl.ds(h * half, half)
        return remote(
            psend.at[pl.ds(pl.multiple_of(peer * sub, sub), sub), columns],
            precv.at[ex, :, columns],
            p_send,
            p_recv.at[h],
            {"exp": peer},
        )

    for h in range(2):

        def project(n, _, h=h):
            columns = pl.ds(pl.multiple_of(h * half + n * tile, tile), tile)
            psend[:, columns] = jnp.dot(
                att[...], ow_v[:, columns], preferred_element_type=F32
            ).astype(BF16)
            return 0

        lax.fori_loop(0, half // tile, project, 0)

        def p_start(s, _, h=h):
            p_copy(h, s).start()
            return 0

        lax.fori_loop(1, n_exp, p_start, 0)

    precv[ex] = psend[pl.ds(pl.multiple_of(ex * sub, sub), sub), :]
    for h in range(2):
        columns = pl.ds(h * half, half)

        arrived(psend.at[pl.ds(0, (n_exp - 1) * sub), columns], p_recv.at[h])
        value = res_v[:, columns].astype(F32)
        for j in range(n_exp):
            value = value + precv[j, :, columns].astype(F32)
        mixed_ref[:, columns] = value

    mixed = mixed_ref[...]
    square = jnp.mean(mixed * mixed, axis=1, keepdims=True)
    normed_ref[...] = (mixed * lax.rsqrt(square + EPS) * gain_v[...].astype(F32)).astype(BF16)

    for copy in kv_copies:
        copy.wait_send()

    arrived(qbuf.at[pl.ds(0, n_chip - 1)], q_send)
    arrived(osend.at[pl.ds(0, n_chip - 1)], o_send)
    arrived(ssend.at[pl.ds(0, n_chip - 1)], s_send)
    arrived(psend.at[pl.ds(0, (n_exp - 1) * sub)], p_send)


def attend(limit, q, nk, nv, ck, cv, res, ow, gain):
    n_ctx, n_exp = lax.axis_size("ctx"), lax.axis_size("exp")
    n_chip = n_ctx // 2
    tok, q_width = q.shape
    cache = ck.shape[0]
    sub, width = res.shape
    rows = 2 * (cache + tok)
    block = (q_width // HD) * tok
    vmem = pl.BlockSpec(memory_space=pltpu.VMEM)
    dma = pltpu.SemaphoreType.DMA
    flops = 4 * n_chip * block * rows * HD + 2 * tok * q_width * width
    return pl.pallas_call(
        functools.partial(attend_kernel, n_ctx, n_exp),
        out_shape=(
            jax.ShapeDtypeStruct((sub, width), BF16),
            jax.ShapeDtypeStruct((sub, width), F32),
        ),
        in_specs=[pl.BlockSpec(memory_space=pltpu.SMEM)]
        + [pl.BlockSpec(memory_space=pl.ANY)] * 8,
        out_specs=(vmem, vmem),
        scratch_shapes=[
            pltpu.VMEM((rows, HD), BF16),
            pltpu.VMEM((rows, HD), BF16),
            pltpu.VMEM((HD, rows), BF16),
            pltpu.VMEM((rows, 2 * HD), BF16),
            pltpu.VMEM((n_chip, block, HD), BF16),
            pltpu.VMEM((n_chip, block, HD), BF16),
            pltpu.VMEM((n_chip, block, HD), BF16),
            pltpu.VMEM((n_chip, 8, tok), F32),
            pltpu.VMEM((n_chip, 8, tok), F32),
            pltpu.VMEM((tok, q_width), BF16),
            pltpu.VMEM((q_width, width), BF16),
            pltpu.VMEM((tok, width), BF16),
            pltpu.VMEM((n_exp, sub, width), BF16),
            pltpu.VMEM((sub, width), BF16),
            pltpu.VMEM((1, width), BF16),
            dma((q_width // HD + 6,)),
            dma((4,)),
            dma((4,)),
            dma,
            dma((n_chip,)),
            dma,
            dma,
            dma,
            dma,
            dma,
            dma((2,)),
            dma,
        ],
        compiler_params=pltpu.CompilerParams(
            collective_id=0, has_side_effects=True, vmem_limit_bytes=60 * 2**20
        ),
        cost_estimate=pl.CostEstimate(
            flops=flops, bytes_accessed=8 * 2**20, transcendentals=n_chip * block * rows
        ),
    )(limit, q, nk, nv, ck, cv, res, ow, gain)


def expert_kernel(
    n_ctx,
    n_exp,
    chunks,
    cap,
    normed_ref,
    wg_ref,
    wu_ref,
    wd_ref,
    ids_ref,
    gates_ref,
    mixed_ref,
    out_ref,
    nbuf,
    sel_v,
    back_v,
    slot_gate,
    mixed_v,
    xall,
    wg_v,
    wu_v,
    wd_v,
    acc_g,
    acc_u,
    hid,
    tbuf,
    sbuf,
    red,
    ybuf,
    xbuf,
    fbuf,
    wsend,
    wrecv,
    wg_sem,
    wu_sem,
    wd_sem,
    in_sem,
    n_send,
    n_recv,
    a_send,
    a_recv,
    r_send,
    r_recv,
    e_send,
    e_recv,
):
    n_y = n_ctx // 4
    me = lax.axis_index("ctx")
    ex = lax.axis_index("exp")
    k = me % 2
    x = me // (2 * n_y)
    y = (me // 2) % n_y
    y_up, y_down, y_far = (y + 1) % n_y, (y + n_y - 1) % n_y, (y + 2) % n_y
    sib = {"ctx": me + 1 - 2 * k}
    across = {"ctx": ((1 - x) * n_y + y) * 2 + k}
    up = {"ctx": (x * n_y + y_up) * 2 + k}
    down = {"ctx": (x * n_y + y_down) * 2 + k}
    far = {"ctx": (x * n_y + y_far) * 2 + k}
    sub, width = out_ref.shape
    tok = sub * n_exp
    total = n_ctx * cap
    side = total // 2
    span = width // chunks
    own_rows = pl.ds(pl.multiple_of(ex * sub, sub), sub)

    def cols(c):
        return pl.ds(pl.multiple_of(c * span, span), span)

    barrier = pltpu.get_barrier_semaphore()
    for where in (sib, across, up, down, far):
        pl.semaphore_signal(barrier, inc=1, device_id=where, device_id_type=MESH)

    def greet_exp(s, _):
        pl.semaphore_signal(
            barrier, inc=1, device_id={"exp": (ex + s) % n_exp}, device_id_type=MESH
        )
        return 0

    lax.fori_loop(1, n_exp, greet_exp, 0)
    own_load = pltpu.make_async_copy(normed_ref, nbuf.at[own_rows], in_sem.at[0])
    own_load.start()
    pl.semaphore_wait(barrier, 4 + n_exp)

    def n_copy(c, s, row_of, peer):
        at = pl.ds(pl.multiple_of(row_of * sub, sub), sub)
        return remote(
            normed_ref.at[:, cols(c)],
            nbuf.at[at, cols(c)],
            n_send,
            n_recv.at[c],
            {"exp": peer},
        )

    def n_start(c, _):
        def one(s, _):
            n_copy(c, s, ex, (ex + s) % n_exp).start()
            return 0

        lax.fori_loop(1, n_exp, one, 0)
        return 0

    lax.fori_loop(0, chunks, n_start, 0)

    def w_copies(c):
        at = pl.ds(pl.multiple_of(c * span, span), span)
        return (
            pltpu.make_async_copy(wg_ref.at[at], wg_v.at[at], wg_sem.at[c]),
            pltpu.make_async_copy(wu_ref.at[at], wu_v.at[at], wu_sem.at[c]),
        )

    def w_start(c, _):
        for copy in w_copies(c):
            copy.start()
        return 0

    lax.fori_loop(0, chunks, w_start, 0)
    wd_copy = pltpu.make_async_copy(wd_ref, wd_v, wd_sem)
    wd_copy.start()
    mixed_copy = pltpu.make_async_copy(mixed_ref, mixed_v, in_sem.at[1])
    mixed_copy.start()

    slots = -(-cap // HD) * HD
    first, second = ids_ref[0:1, :] == ex, ids_ref[1:2, :] == ex
    hit = jnp.where(first, 1.0, 0.0) + jnp.where(second, 1.0, 0.0)
    weight = jnp.where(first, gates_ref[0:1, :], 0.0) + jnp.where(second, gates_ref[1:2, :], 0.0)
    earlier = lax.broadcasted_iota(jnp.int32, (tok, tok), 0) <= lax.broadcasted_iota(
        jnp.int32, (tok, tok), 1
    )
    count = jnp.dot(
        jnp.broadcast_to(hit, (16, tok)).astype(BF16),
        jnp.where(earlier, 1.0, 0.0).astype(BF16),
        preferred_element_type=F32,
    )
    place = lax.broadcasted_iota(jnp.int32, (slots, tok), 0).astype(F32)
    chosen = jnp.where(place == count[0:1, :] - 1.0, hit, 0.0)
    sel_v[...] = chosen[0:cap, :].astype(BF16)
    back_v[...] = chosen.T[:, 0:cap].astype(BF16)
    slot_gate[...] = jnp.sum(chosen * weight, axis=1, keepdims=True)[0:cap, :]
    acc_g[...] = jnp.zeros_like(acc_g)
    acc_u[...] = jnp.zeros_like(acc_u)
    own_load.wait()

    half = chunks // 2

    def gather(kind, c, at, where):
        ref = xall.at[(c, *at)]
        return remote(ref, ref, a_send.at[kind], a_recv.at[min(kind, 3), c], where)

    def a_own(c):
        return [gather(0, c, (k, x, y), where) for where in (up, down, far)]

    def a_pass(c):
        return [gather(1, c, (k, 1 - x, y), where) for where in (up, down, far)]

    def a_block(c):
        return gather(2, c, (k, x, y), across)

    def a_plane(c):
        ref = xall.at[c, k, x]
        return remote(ref, ref, a_send.at[4], a_recv.at[2, c], across)

    def a_sib(c, plane):
        return gather(3, c, (k, plane), sib)

    three = pl.ds(0, 3)

    def gather_step(it, _):
        @pl.when(it < chunks)
        def _():
            c = it

            arrived(nbuf.at[pl.ds(0, (n_exp - 1) * sub), cols(c)], n_recv.at[c])
            xall[c, k, x, y] = jnp.dot(
                sel_v[...], nbuf[:, cols(c)], preferred_element_type=F32
            ).astype(BF16)

            @pl.when(c % 2 == 0)
            def _():
                a_block(c).start()

            for copy in a_own(c):
                copy.start()

        @pl.when((it >= 2) & (it < chunks + 2))
        def _():
            c = it - 2

            @pl.when(c % 2 == 0)
            def _():
                arrived(xall.at[c, k, 1 - x, y], a_recv.at[2, c])
                for copy in a_pass(c):
                    copy.start()
                arrived(xall.at[c, k, x, three], a_recv.at[0, c])

            @pl.when(c % 2 == 1)
            def _():
                arrived(xall.at[c, k, x, three], a_recv.at[0, c])
                a_plane(c).start()

            a_sib(c, x).start()

        @pl.when((it >= 4) & (it < chunks + 4))
        def _():
            c = it - 4

            @pl.when(c % 2 == 0)
            def _():
                arrived(xall.at[c, k, 1 - x, three], a_recv.at[1, c])

            @pl.when(c % 2 == 1)
            def _():
                arrived(xall.at[c, k, 1 - x], a_recv.at[2, c])

            a_sib(c, 1 - x).start()

        @pl.when(it >= 5)
        def _():
            c = it - 5
            arrived(xall.at[c, 1 - k], a_recv.at[3, c])
            for copy in w_copies(c):
                copy.wait()
            lhs = xall[c].reshape(total, span)
            acc_g[...] += jnp.dot(lhs, wg_v[cols(c), :], preferred_element_type=F32)
            acc_u[...] += jnp.dot(lhs, wu_v[cols(c), :], preferred_element_type=F32)

        return 0

    lax.fori_loop(0, chunks + 5, gather_step, 0)

    gate = acc_g[...]
    hid[...] = (gate / (1.0 + jnp.exp(-gate)) * acc_u[...]).astype(BF16)
    wd_copy.wait()
    mixed_copy.wait()

    def reduce(kind, c, src, dst, where):
        return remote(src, dst, r_send.at[kind], r_recv.at[kind, c], where)

    def r_sib(c):
        return reduce(0, c, tbuf.at[c], sbuf.at[c], sib)

    def r_pairs(c):
        return (
            reduce(1, c, red.at[c, :, y_up], ybuf.at[c // 2, 0], up),
            reduce(1, c, red.at[c, :, y_down], ybuf.at[c // 2, 1], down),
            reduce(1, c, red.at[c, :, y_far], ybuf.at[c // 2, 2], far),
        )

    def r_block(c):
        return reduce(2, c, red.at[c, 1 - x, y], fbuf.at[c, 0], across)

    def r_plane(c):
        return reduce(3, c, red.at[c, 1 - x], xbuf.at[c // 2], across)

    def r_own(c):
        return (
            reduce(4, c, red.at[c, x, y_up], fbuf.at[c, 0], up),
            reduce(4, c, red.at[c, x, y_down], fbuf.at[c, 1], down),
            reduce(4, c, red.at[c, x, y_far], fbuf.at[c, 2], far),
        )

    def e_copy(c, s, row_of, slot, peer):
        at = pl.ds(pl.multiple_of(row_of * sub, sub), sub)
        return remote(
            wsend.at[at, cols(c)],
            wrecv.at[slot, :, cols(c)],
            e_send,
            e_recv.at[c],
            {"exp": peer},
        )

    other_half = pl.ds(pl.multiple_of((1 - k) * side, 16), side)
    own_half = pl.ds(pl.multiple_of(k * side, 16), side)
    shape = (2, n_y, cap, span)

    def reduce_step(it, _):
        @pl.when(it < chunks)
        def _():
            c = it
            tbuf[c] = (
                jnp.dot(hid[other_half, :], wd_v[:, cols(c)], preferred_element_type=F32)
                .astype(BF16)
                .reshape(shape)
            )
            r_sib(c).start()
            red[c] = (
                jnp.dot(hid[own_half, :], wd_v[:, cols(c)], preferred_element_type=F32)
                .astype(BF16)
                .reshape(shape)
            )

        @pl.when((it >= 1) & (it < chunks + 1))
        def _():
            c = it - 1
            arrived(sbuf.at[c], r_recv.at[0, c])
            red[c] = (red[c].astype(F32) + sbuf[c].astype(F32)).astype(BF16)

            @pl.when(c % 2 == 0)
            def _():
                for copy in r_pairs(c):
                    copy.start()

            @pl.when(c % 2 == 1)
            def _():
                r_plane(c).start()

        @pl.when((it >= 3) & (it < chunks + 3))
        def _():
            c = it - 3

            @pl.when(c % 2 == 0)
            def _():
                arrived(ybuf.at[c // 2], r_recv.at[1, c])
                for px in range(2):
                    value = red[c, px, y].astype(F32)
                    for i in range(3):
                        value = value + ybuf[c // 2, i, px].astype(F32)
                    red[c, px, y] = value.astype(BF16)
                r_block(c).start()

            @pl.when(c % 2 == 1)
            def _():
                arrived(xbuf.at[c // 2], r_recv.at[3, c])
                red[c, x] = (red[c, x].astype(F32) + xbuf[c // 2].astype(F32)).astype(BF16)
                for copy in r_own(c):
                    copy.start()

        @pl.when((it >= 5) & (it < chunks + 5))
        def _():
            c = it - 5

            @pl.when(c % 2 == 0)
            def _():
                arrived(fbuf.at[c, 0], r_recv.at[2, c])
                value = red[c, x, y].astype(F32) + fbuf[c, 0].astype(F32)
                red[c, x, y] = value.astype(BF16)

            @pl.when(c % 2 == 1)
            def _():
                arrived(fbuf.at[c], r_recv.at[4, c])
                value = red[c, x, y].astype(F32)
                for i in range(3):
                    value = value + fbuf[c, i].astype(F32)
                red[c, x, y] = value.astype(BF16)

            scaled = (slot_gate[...] * red[c, x, y].astype(F32)).astype(BF16)
            wsend[:, cols(c)] = jnp.dot(
                back_v[...], scaled, preferred_element_type=F32
            ).astype(BF16)

            def start(s, _):
                peer = (ex + s) % n_exp
                e_copy(c, s, peer, ex, peer).start()
                return 0

            lax.fori_loop(1, n_exp, start, 0)
            wrecv[ex, :, cols(c)] = wsend[own_rows, cols(c)]

        @pl.when(it >= 7)
        def _():
            c = it - 7

            arrived(wsend.at[pl.ds(0, (n_exp - 1) * sub), cols(c)], e_recv.at[c])
            value = mixed_v[:, cols(c)]
            for j in range(n_exp):
                value = value + wrecv[j, :, cols(c)].astype(F32)
            out_ref[:, cols(c)] = value.astype(BF16)

        return 0

    lax.fori_loop(0, chunks + 7, reduce_step, 0)

    few = pl.ds(0, half)
    for i, ref in enumerate(
        [
            xall.at[:, 0, 0, three],
            xall.at[few, 0, 0, three],
            xall.at[few, 0, 0, 0],
            xall.at[:, 0],
            xall.at[few, 0, 0],
        ]
    ):
        arrived(ref, a_send.at[i])
    for i, ref in enumerate([tbuf, ybuf, fbuf.at[few, 0], xbuf, fbuf.at[few]]):
        arrived(ref, r_send.at[i])
    others = pl.ds(0, (n_exp - 1) * sub)
    arrived(nbuf.at[others], n_send)
    arrived(wsend.at[others], e_send)


def experts(normed, wg, wu, wd, ids, gates, mixed):
    n_ctx, n_exp = lax.axis_size("ctx"), lax.axis_size("exp")
    sub, width = normed.shape
    hidden = wg.shape[1]
    tok = ids.shape[1]
    cap = 3 * tok // n_exp
    chunks = 8
    span = width // chunks
    total = n_ctx * cap
    n_y = n_ctx // 4
    vmem = pl.BlockSpec(memory_space=pltpu.VMEM)
    hbm = pl.BlockSpec(memory_space=pl.ANY)
    dma = pltpu.SemaphoreType.DMA
    return pl.pallas_call(
        functools.partial(expert_kernel, n_ctx, n_exp, chunks, cap),
        out_shape=jax.ShapeDtypeStruct((sub, width), BF16),
        in_specs=[hbm, hbm, hbm, hbm, vmem, vmem, hbm],
        out_specs=vmem,
        scratch_shapes=[
            pltpu.VMEM((tok, width), BF16),
            pltpu.VMEM((cap, tok), BF16),
            pltpu.VMEM((tok, cap), BF16),
            pltpu.VMEM((cap, 1), F32),
            pltpu.VMEM((sub, width), F32),
            pltpu.VMEM((chunks, 2, 2, n_y, cap, span), BF16),
            pltpu.VMEM((width, hidden), BF16),
            pltpu.VMEM((width, hidden), BF16),
            pltpu.VMEM((hidden, width), BF16),
            pltpu.VMEM((total, hidden), F32),
            pltpu.VMEM((total, hidden), F32),
            pltpu.VMEM((total, hidden), BF16),
            pltpu.VMEM((chunks, 2, n_y, cap, span), BF16),
            pltpu.VMEM((chunks, 2, n_y, cap, span), BF16),
            pltpu.VMEM((chunks, 2, n_y, cap, span), BF16),
            pltpu.VMEM((chunks // 2, 3, 2, cap, span), BF16),
            pltpu.VMEM((chunks // 2, n_y, cap, span), BF16),
            pltpu.VMEM((chunks, 3, cap, span), BF16),
            pltpu.VMEM((tok, width), BF16),
            pltpu.VMEM((n_exp, sub, width), BF16),
            dma((chunks,)),
            dma((chunks,)),
            dma,
            dma((2,)),
            dma,
            dma((chunks,)),
            dma((5,)),
            dma((4, chunks)),
            dma((5,)),
            dma((5, chunks)),
            dma,
            dma((chunks,)),
        ],
        compiler_params=pltpu.CompilerParams(
            collective_id=1, has_side_effects=True, vmem_limit_bytes=60 * 2**20
        ),
        cost_estimate=pl.CostEstimate(
            flops=6 * total * width * hidden,
            bytes_accessed=6 * width * hidden,
            transcendentals=total * hidden,
        ),
    )(normed, wg, wu, wd, ids, gates, mixed)


def local(
    queries,
    new_keys,
    new_values,
    cache_keys,
    cache_values,
    cache_length,
    residual,
    out_weight,
    norm_gain,
    route_ids,
    route_gates,
    w_gate,
    w_up,
    w_down,
):
    normed, own_mixed = attend(
        cache_length,
        queries,
        new_keys,
        new_values,
        cache_keys,
        cache_values,
        residual,
        out_weight,
        norm_gain[None, :],
    )
    return experts(
        normed, w_gate[0], w_up[0], w_down[0], route_ids.T, route_gates.T, own_mixed
    )


def solution(mesh):
    placed = (
        P("ctx", "exp"),
        P("ctx", "exp"),
        P("ctx", "exp"),
        P("ctx", "exp"),
        P("ctx", "exp"),
        P(),
        P(("ctx", "exp"), None),
        P("exp", None),
        P(),
        P("ctx", None),
        P("ctx", None),
        P("exp", None, "ctx"),
        P("exp", None, "ctx"),
        P("exp", "ctx", None),
    )
    return jax.shard_map(
        local, mesh=mesh, in_specs=placed, out_specs=P(("ctx", "exp"), None), check_vma=False
    )
```

```python
import functools
import math

import jax
import jax.numpy as jnp
from jax import lax
from jax.experimental import pallas as pl
from jax.experimental.pallas import tpu as pltpu
from jax.sharding import PartitionSpec as P

HD = 128
NEG = -1e30
EPS = 1e-05
MESH = pl.DeviceIdType.MESH
F32 = jnp.float32
BF16 = jnp.bfloat16


def remote(src, dst, send, recv, where):
    return pltpu.make_async_remote_copy(
        src_ref=src,
        dst_ref=dst,
        send_sem=send,
        recv_sem=recv,
        device_id=where,
        device_id_type=MESH,
    )


def arrived(ref, sem):
    pltpu.make_async_copy(ref, ref, sem).wait()


def attend_kernel(
    n_ctx,
    n_exp,
    limit_ref,
    q_ref,
    nk_ref,
    nv_ref,
    ck_ref,
    cv_ref,
    res_ref,
    ow_ref,
    gain_ref,
    normed_ref,
    mixed_ref,
    prepare,
    load_weights,
    kbuf,
    vbuf,
    kt,
    vext,
    qbuf,
    osend,
    orecv,
    ssend,
    srecv,
    att,
    ow_v,
    psend,
    precv,
    res_v,
    gain_v,
    in_sem,
    kv_send,
    kv_recv,
    q_send,
    q_recv,
    o_send,
    o_recv,
    s_send,
    s_recv,
    p_send,
    p_recv,
    ow_sem,
):
    n_chip = n_ctx // 2
    me = lax.axis_index("ctx")
    ex = lax.axis_index("exp")
    chip = me // 2
    core = me % 2
    sib = me + 1 - 2 * core
    tok = q_ref.shape[0]
    group = q_ref.shape[1] // HD
    cache = ck_ref.shape[0]
    sub, width = res_ref.shape
    c_all = 2 * cache
    rows = c_all + 2 * tok

    ow_copy = pltpu.make_async_copy(ow_ref, ow_v, ow_sem)
    barrier = pltpu.get_barrier_semaphore()

    def greet_chip(s, _):
        peer = ((chip + s) % n_chip) * 2 + core
        pl.semaphore_signal(barrier, inc=1, device_id={"ctx": peer}, device_id_type=MESH)
        return 0

    def greet_exp(s, _):
        pl.semaphore_signal(
            barrier, inc=1, device_id={"exp": (ex + s) % n_exp}, device_id_type=MESH
        )
        return 0

    pl.semaphore_signal(barrier, inc=1, device_id={"ctx": sib}, device_id_type=MESH)
    lax.fori_loop(1, n_chip, greet_chip, 0)
    lax.fori_loop(1, n_exp, greet_exp, 0)

    moves = [
        (q_ref.at[:, pl.ds(g * HD, HD)], qbuf.at[chip, pl.ds(g * tok, tok)]) for g in range(group)
    ]
    moves += [
        (ck_ref, kbuf.at[pl.ds(0, cache)]),
        (nk_ref, kbuf.at[pl.ds(c_all, tok)]),
        (cv_ref, vbuf.at[pl.ds(0, cache)]),
        (nv_ref, vbuf.at[pl.ds(c_all, tok)]),
        (res_ref, res_v),
        (gain_ref, gain_v),
    ]
    loads = [pltpu.make_async_copy(a, b, in_sem.at[i]) for i, (a, b) in enumerate(moves)]
    for load in loads:
        load.start()
    for load in loads[0:group]:
        load.wait()
    prepare()
    pl.semaphore_wait(barrier, n_chip + n_exp - 1)

    kv_copies = [
        remote(src, dst, kv_send.at[i], kv_recv.at[i], {"ctx": sib})
        for i, (src, dst) in enumerate(
            [
                (ck_ref, kbuf.at[pl.ds(cache, cache)]),
                (nk_ref, kbuf.at[pl.ds(c_all + tok, tok)]),
                (cv_ref, vbuf.at[pl.ds(cache, cache)]),
                (nv_ref, vbuf.at[pl.ds(c_all + tok, tok)]),
            ]
        )
    ]
    for copy in kv_copies:
        copy.start()

    def q_copy(s):
        peer = ((chip + n_chip - s) % n_chip) * 2 + core
        return remote(
            qbuf.at[chip], qbuf.at[chip], q_send, q_recv.at[chip], {"ctx": peer}
        )

    def q_start(s, _):
        q_copy(s).start()
        return 0

    lax.fori_loop(1, n_chip, q_start, 0)
    ow_copy.start()
    load_weights()
    for load in loads[group:]:
        load.wait()

    for copy in kv_copies:
        copy.wait_recv()
    kt[...] = kbuf[...].T
    vext[:, 0:HD] = vbuf[...]
    vext[:, HD : 2 * HD] = jnp.ones((rows, HD), BF16)

    limit = limit_ref[0]
    position = lax.broadcasted_iota(jnp.int32, (1, cache), 1)
    bias_own = jnp.where(position + me * cache < limit, 0.0, NEG)
    bias_sib = jnp.where(position + sib * cache < limit, 0.0, NEG)
    cache_bias = jnp.concatenate([bias_own, bias_sib], axis=1)
    t_row = lax.broadcasted_iota(jnp.int32, (tok, 2 * tok), 0)
    t_col = lax.broadcasted_iota(jnp.int32, (tok, 2 * tok), 1)
    lane = lax.broadcasted_iota(jnp.int32, (tok, HD), 1)
    key_at = jnp.where(t_col < tok, t_col + me * tok, t_col - tok + sib * tok)
    scale = math.log2(math.e) / math.sqrt(HD)

    def o_copy(s, src):
        peer = src * 2 + core
        return (
            remote(osend.at[s], orecv.at[chip], o_send, o_recv, {"ctx": peer}),
            remote(ssend.at[s], srecv.at[chip], s_send, s_recv, {"ctx": peer}),
        )

    def step(s, _):
        src = (chip + s) % n_chip

        @pl.when(s > 0)
        def _():
            arrived(qbuf.at[src], q_recv.at[src])

        query_at = t_row + (src * 2 + core) * tok
        new_bias = jnp.where(key_at <= query_at, 0.0, NEG)
        stat = jnp.zeros((tok, HD), F32)
        for g in range(group):
            q = qbuf[src, g * tok : (g + 1) * tok, :]
            sc = jnp.dot(q, kt[:, 0:c_all], preferred_element_type=F32) * scale + cache_bias
            sn = jnp.dot(q, kt[:, c_all:rows], preferred_element_type=F32) * scale + new_bias
            top = jnp.maximum(
                jnp.max(sc, axis=1, keepdims=True), jnp.max(sn, axis=1, keepdims=True)
            )
            pc = jnp.exp2(sc - top).astype(BF16)
            pn = jnp.exp2(sn - top).astype(BF16)
            o = jnp.dot(pc, vext[0:c_all, :], preferred_element_type=F32) + jnp.dot(
                pn, vext[c_all:rows, :], preferred_element_type=F32
            )
            total = o[:, HD : 2 * HD]
            osend[s, g * tok : (g + 1) * tok, :] = (o[:, 0:HD] / total).astype(BF16)
            stat = jnp.where(lane == g, top + jnp.log2(total), stat)
        ssend[s] = stat.T[0:8, :]

        @pl.when(s > 0)
        def _():
            for copy in o_copy(s, src):
                copy.start()

        return 0

    lax.fori_loop(0, n_chip, step, 0)
    orecv[chip] = osend[0]
    srecv[chip] = ssend[0]

    arrived(orecv.at[pl.ds(0, n_chip - 1)], o_recv)
    arrived(srecv.at[pl.ds(0, n_chip - 1)], s_recv)

    stats = srecv[...]
    peak = jnp.max(stats, axis=0, keepdims=True)
    share = jnp.exp2(stats - peak)
    share = share / jnp.sum(share, axis=0, keepdims=True)
    share = share.reshape(n_chip * 8, tok)
    if n_chip * 8 < HD:
        share = jnp.concatenate([share, jnp.zeros((HD - n_chip * 8, tok), F32)], axis=0)
    share = share.T
    for g in range(group):
        value = jnp.zeros((tok, HD), F32)
        for i in range(n_chip):
            part = orecv[i, g * tok : (g + 1) * tok, :].astype(F32)
            value = value + share[:, i * 8 + g : i * 8 + g + 1] * part
        att[:, g * HD : (g + 1) * HD] = value.astype(BF16)

    ow_copy.wait()
    half = width // 2
    tile = min(512, half)

    def p_copy(h, s):
        peer = (ex + s) % n_exp
        columns = pl.ds(h * half, half)
        return remote(
            psend.at[pl.ds(pl.multiple_of(peer * sub, sub), sub), columns],
            precv.at[ex, :, columns],
            p_send,
            p_recv.at[h],
            {"exp": peer},
        )

    for h in range(2):

        def project(n, _, h=h):
            columns = pl.ds(pl.multiple_of(h * half + n * tile, tile), tile)
            psend[:, columns] = jnp.dot(
                att[...], ow_v[:, columns], preferred_element_type=F32
            ).astype(BF16)
            return 0

        lax.fori_loop(0, half // tile, project, 0)

        def p_start(s, _, h=h):
            p_copy(h, s).start()
            return 0

        lax.fori_loop(1, n_exp, p_start, 0)

    precv[ex] = psend[pl.ds(pl.multiple_of(ex * sub, sub), sub), :]
    for h in range(2):
        columns = pl.ds(h * half, half)

        arrived(psend.at[pl.ds(0, (n_exp - 1) * sub), columns], p_recv.at[h])
        value = res_v[:, columns].astype(F32)
        for j in range(n_exp):
            value = value + precv[j, :, columns].astype(F32)
        mixed_ref[:, columns] = value

    mixed = mixed_ref[...]
    square = jnp.mean(mixed * mixed, axis=1, keepdims=True)
    normed_ref[...] = (mixed * lax.rsqrt(square + EPS) * gain_v[...].astype(F32)).astype(BF16)

    def drain():
        for copy in kv_copies:
            copy.wait_send()
        arrived(qbuf.at[pl.ds(0, n_chip - 1)], q_send)
        arrived(osend.at[pl.ds(0, n_chip - 1)], o_send)
        arrived(ssend.at[pl.ds(0, n_chip - 1)], s_send)
        arrived(psend.at[pl.ds(0, (n_exp - 1) * sub)], p_send)

    return drain


def select_slots(ids_ref, gates_ref, sel_v, back_v, slot_gate):
    ex = lax.axis_index("exp")
    cap, tok = sel_v.shape
    slots = -(-cap // HD) * HD
    first, second = ids_ref[0:1, :] == ex, ids_ref[1:2, :] == ex
    hit = jnp.where(first, 1.0, 0.0) + jnp.where(second, 1.0, 0.0)
    weight = jnp.where(first, gates_ref[0:1, :], 0.0) + jnp.where(second, gates_ref[1:2, :], 0.0)
    earlier = lax.broadcasted_iota(jnp.int32, (tok, tok), 0) <= lax.broadcasted_iota(
        jnp.int32, (tok, tok), 1
    )
    count = jnp.dot(
        jnp.broadcast_to(hit, (16, tok)).astype(BF16),
        jnp.where(earlier, 1.0, 0.0).astype(BF16),
        preferred_element_type=F32,
    )
    place = lax.broadcasted_iota(jnp.int32, (slots, tok), 0).astype(F32)
    chosen = jnp.where(place == count[0:1, :] - 1.0, hit, 0.0)
    sel_v[...] = chosen[0:cap, :].astype(BF16)
    back_v[...] = chosen.T[:, 0:cap].astype(BF16)
    slot_gate[...] = jnp.sum(chosen * weight, axis=1, keepdims=True)[0:cap, :]


def expert_kernel(
    n_ctx,
    n_exp,
    chunks,
    waves,
    cap,
    w_copies,
    wd_copy,
    normed_ref,
    out_ref,
    nbuf,
    sel_v,
    back_v,
    slot_gate,
    mixed_v,
    xall,
    wg_v,
    wu_v,
    wd_v,
    acc_g,
    acc_u,
    hid,
    tbuf,
    sbuf,
    dbuf,
    ybuf,
    xbuf,
    fbuf,
    wsend,
    wrecv,
    n_send,
    n_recv,
    a_send,
    a_recv,
    r_send,
    r_recv,
    e_send,
    e_recv,
):
    n_y = n_ctx // 4
    me = lax.axis_index("ctx")
    ex = lax.axis_index("exp")
    k = me % 2
    x = me // (2 * n_y)
    y = (me // 2) % n_y
    y_up, y_down, y_far = (y + 1) % n_y, (y + n_y - 1) % n_y, (y + 2) % n_y
    sib = {"ctx": me + 1 - 2 * k}
    across = {"ctx": ((1 - x) * n_y + y) * 2 + k}
    up = {"ctx": (x * n_y + y_up) * 2 + k}
    down = {"ctx": (x * n_y + y_down) * 2 + k}
    far = {"ctx": (x * n_y + y_far) * 2 + k}
    sub, width = out_ref.shape
    tok = sub * n_exp
    total = n_ctx * cap
    part = cap // waves
    steps = waves * chunks
    span = width // chunks
    own_rows = pl.ds(pl.multiple_of(ex * sub, sub), sub)

    def cols(c):
        return pl.ds(pl.multiple_of(c * span, span), span)

    nbuf[own_rows, :] = normed_ref[...]

    def n_copy(c, s, row_of, peer):
        at = pl.ds(pl.multiple_of(row_of * sub, sub), sub)
        return remote(
            normed_ref.at[:, cols(c)],
            nbuf.at[at, cols(c)],
            n_send,
            n_recv.at[c],
            {"exp": peer},
        )

    def n_start(c, _):
        def one(s, _):
            n_copy(c, s, ex, (ex + s) % n_exp).start()
            return 0

        lax.fori_loop(1, n_exp, one, 0)
        return 0

    lax.fori_loop(0, chunks, n_start, 0)

    half = steps // 2

    def gather(kind, c, at, where):
        ref = xall.at[(c, *at)]
        return remote(ref, ref, a_send.at[kind], a_recv.at[min(kind, 3), c], where)

    def a_own(c):
        return [gather(0, c, (k, x, y), where) for where in (up, down, far)]

    def a_pass(c):
        return [gather(1, c, (k, 1 - x, y), where) for where in (up, down, far)]

    def a_block(c):
        return gather(2, c, (k, x, y), across)

    def a_plane(c):
        ref = xall.at[c, k, x]
        return remote(ref, ref, a_send.at[4], a_recv.at[2, c], across)

    def a_sib(c, plane):
        return gather(3, c, (k, plane), sib)

    three = pl.ds(0, 3)

    def reduce(kind, c, src, dst, where):
        return remote(src, dst, r_send.at[kind], r_recv.at[kind, c], where)

    def r_sib(c):
        return reduce(0, c, tbuf.at[c, 1 - k], sbuf.at[c], sib)

    def r_pairs(c):
        return (
            reduce(1, c, tbuf.at[c, k, :, y_up], ybuf.at[c // 2, 0], up),
            reduce(1, c, tbuf.at[c, k, :, y_down], ybuf.at[c // 2, 1], down),
            reduce(1, c, tbuf.at[c, k, :, y_far], ybuf.at[c // 2, 2], far),
        )

    def r_block(c):
        return reduce(2, c, tbuf.at[c, k, 1 - x, y], fbuf.at[c, 0], across)

    def r_plane(c):
        return reduce(3, c, tbuf.at[c, k, 1 - x], xbuf.at[c // 2], across)

    def r_own(c):
        return (
            reduce(4, c, tbuf.at[c, k, x, y_up], fbuf.at[c, 0], up),
            reduce(4, c, tbuf.at[c, k, x, y_down], fbuf.at[c, 1], down),
            reduce(4, c, tbuf.at[c, k, x, y_far], fbuf.at[c, 2], far),
        )

    def e_copy(c, s, row_of, slot, peer):
        at = pl.ds(pl.multiple_of(row_of * sub, sub), sub)
        return remote(
            wsend.at[at, cols(c)],
            wrecv.at[slot, :, cols(c)],
            e_send,
            e_recv.at[c],
            {"exp": peer},
        )

    def wave_rows(i):
        return pl.ds(pl.multiple_of(i // chunks * part, part), part)

    def step(it, _):
        @pl.when(it < chunks)
        def _():
            arrived(nbuf.at[pl.ds(0, (n_exp - 1) * sub), cols(it)], n_recv.at[it])

        @pl.when(it < steps)
        def _():
            i = it
            xall[i, k, x, y] = jnp.dot(
                sel_v[wave_rows(i), :], nbuf[:, cols(i % chunks)], preferred_element_type=F32
            ).astype(BF16)

            @pl.when(i % 2 == 0)
            def _():
                a_block(i).start()

            for copy in a_own(i):
                copy.start()

        @pl.when((it >= 2) & (it < steps + 2))
        def _():
            i = it - 2

            @pl.when(i % 2 == 0)
            def _():
                arrived(xall.at[i, k, 1 - x, y], a_recv.at[2, i])
                for copy in a_pass(i):
                    copy.start()
                arrived(xall.at[i, k, x, three], a_recv.at[0, i])

            @pl.when(i % 2 == 1)
            def _():
                arrived(xall.at[i, k, x, three], a_recv.at[0, i])
                a_plane(i).start()

            a_sib(i, x).start()

        @pl.when((it >= 4) & (it < steps + 4))
        def _():
            i = it - 4

            @pl.when(i % 2 == 0)
            def _():
                arrived(xall.at[i, k, 1 - x, three], a_recv.at[1, i])

            @pl.when(i % 2 == 1)
            def _():
                arrived(xall.at[i, k, 1 - x], a_recv.at[2, i])

            a_sib(i, 1 - x).start()

        r = it - (chunks + 5)

        @pl.when((r >= 1) & (r < steps + 1))
        def _():
            i = r - 1
            arrived(sbuf.at[i], r_recv.at[0, i])
            tbuf[i, k] = (tbuf[i, k].astype(F32) + sbuf[i].astype(F32)).astype(BF16)

            @pl.when(i % 2 == 0)
            def _():
                for copy in r_pairs(i):
                    copy.start()

            @pl.when(i % 2 == 1)
            def _():
                r_plane(i).start()

        @pl.when((r >= 3) & (r < steps + 3))
        def _():
            i = r - 3

            @pl.when(i % 2 == 0)
            def _():
                arrived(ybuf.at[i // 2], r_recv.at[1, i])
                for px in range(2):
                    value = tbuf[i, k, px, y].astype(F32)
                    for j in range(3):
                        value = value + ybuf[i // 2, j, px].astype(F32)
                    tbuf[i, k, px, y] = value.astype(BF16)
                r_block(i).start()

            @pl.when(i % 2 == 1)
            def _():
                arrived(xbuf.at[i // 2], r_recv.at[3, i])
                tbuf[i, k, x] = (tbuf[i, k, x].astype(F32) + xbuf[i // 2].astype(F32)).astype(BF16)
                for copy in r_own(i):
                    copy.start()

        @pl.when((r >= 5) & (r < steps + 5))
        def _():
            i = r - 5
            c = i % chunks

            @pl.when(i % 2 == 0)
            def _():
                arrived(fbuf.at[i, 0], r_recv.at[2, i])
                value = tbuf[i, k, x, y].astype(F32) + fbuf[i, 0].astype(F32)
                tbuf[i, k, x, y] = value.astype(BF16)

            @pl.when(i % 2 == 1)
            def _():
                arrived(fbuf.at[i], r_recv.at[4, i])
                value = tbuf[i, k, x, y].astype(F32)
                for j in range(3):
                    value = value + fbuf[i, j].astype(F32)
                tbuf[i, k, x, y] = value.astype(BF16)

            scaled = slot_gate[wave_rows(i), :] * tbuf[i, k, x, y].astype(F32)
            dbuf[wave_rows(i), cols(c)] = scaled.astype(BF16)

            @pl.when(i >= steps - chunks)
            def _():
                wsend[:, cols(c)] = jnp.dot(
                    back_v[...], dbuf[:, cols(c)], preferred_element_type=F32
                ).astype(BF16)

                def start(s, _):
                    peer = (ex + s) % n_exp
                    e_copy(c, s, peer, ex, peer).start()
                    return 0

                lax.fori_loop(1, n_exp, start, 0)
                wrecv[ex, :, cols(c)] = wsend[own_rows, cols(c)]

        @pl.when(r >= steps - chunks + 7)
        def _():
            c = (r - 7) % chunks
            arrived(wsend.at[pl.ds(0, (n_exp - 1) * sub), cols(c)], e_recv.at[c])
            value = mixed_v[:, cols(c)]
            for j in range(n_exp):
                value = value + wrecv[j, :, cols(c)].astype(F32)
            out_ref[:, cols(c)] = value.astype(BF16)

        @pl.when(r == 0)
        def _():
            wd_copy.wait()

        @pl.when((r >= 0) & (r < steps))
        def _():
            i = r
            tbuf[i] = (
                jnp.dot(hid[...], wd_v[:, cols(i % chunks)], preferred_element_type=F32)
                .astype(BF16)
                .reshape(2, 2, n_y, part, span)
            )
            r_sib(i).start()

        @pl.when((it >= 5) & (it < chunks + 5))
        def _():
            for copy in w_copies(it - 5):
                copy.wait()

        @pl.when((it >= 5) & (it < steps + 5))
        def _():
            i = it - 5
            c = i % chunks
            arrived(xall.at[i, 1 - k], a_recv.at[3, i])

            @pl.when(c == 0)
            def _():
                acc_g[...] = jnp.zeros_like(acc_g)
                acc_u[...] = jnp.zeros_like(acc_u)

            lhs = xall[i].reshape(total // waves, span)
            acc_g[...] += jnp.dot(lhs, wg_v[cols(c), :], preferred_element_type=F32)
            acc_u[...] += jnp.dot(lhs, wu_v[cols(c), :], preferred_element_type=F32)

            @pl.when(c == chunks - 1)
            def _():
                gate = acc_g[...]
                hid[...] = (gate / (1.0 + jnp.exp(-gate)) * acc_u[...]).astype(BF16)

        return 0

    lax.fori_loop(0, steps + chunks + 12, step, 0)

    few = pl.ds(0, half)
    for i, ref in enumerate(
        [
            xall.at[:, 0, 0, three],
            xall.at[few, 0, 0, three],
            xall.at[few, 0, 0, 0],
            xall.at[:, 0],
            xall.at[few, 0, 0],
        ]
    ):
        arrived(ref, a_send.at[i])
    for i, ref in enumerate([sbuf, ybuf, fbuf.at[few, 0], xbuf, fbuf.at[few]]):
        arrived(ref, r_send.at[i])
    others = pl.ds(0, (n_exp - 1) * sub)
    arrived(nbuf.at[others], n_send)
    arrived(wsend.at[others], e_send)


def layer_kernel(
    n_ctx,
    n_exp,
    chunks,
    waves,
    cap,
    limit_ref,
    q_ref,
    nk_ref,
    nv_ref,
    ck_ref,
    cv_ref,
    res_ref,
    ow_ref,
    gain_ref,
    wg_ref,
    wu_ref,
    wd_ref,
    ids_ref,
    gates_ref,
    out_ref,
    kbuf,
    vbuf,
    kt,
    vext,
    qbuf,
    osend,
    orecv,
    ssend,
    srecv,
    att,
    psend,
    precv,
    res_v,
    gain_v,
    in_sem,
    kv_send,
    kv_recv,
    q_send,
    q_recv,
    o_send,
    o_recv,
    s_send,
    s_recv,
    p_send,
    p_recv,
    ow_sem,
    normed_v,
    nbuf,
    sel_v,
    back_v,
    slot_gate,
    mixed_v,
    xall,
    wg_v,
    wu_v,
    wd_v,
    acc_g,
    acc_u,
    hid,
    tbuf,
    sbuf,
    dbuf,
    ybuf,
    xbuf,
    fbuf,
    wsend,
    wrecv,
    n_send,
    n_recv,
    a_send,
    a_recv,
    r_send,
    r_recv,
    e_send,
    e_recv,
    wg_sem,
    wu_sem,
    wd_sem,
):
    span = wg_ref.shape[0] // chunks

    def w_copies(c):
        at = pl.ds(pl.multiple_of(c * span, span), span)
        return (
            pltpu.make_async_copy(wg_ref.at[at], wg_v.at[at], wg_sem.at[c]),
            pltpu.make_async_copy(wu_ref.at[at], wu_v.at[at], wu_sem.at[c]),
        )

    def load_weights():
        def one(c, _):
            for copy in w_copies(c):
                copy.start()
            return 0

        lax.fori_loop(0, chunks, one, 0)

    def prepare():
        select_slots(ids_ref, gates_ref, sel_v, back_v, slot_gate)

    ow_v = wd_v.at[pl.ds(0, ow_ref.shape[0])]
    drain = attend_kernel(
        n_ctx,
        n_exp,
        limit_ref,
        q_ref,
        nk_ref,
        nv_ref,
        ck_ref,
        cv_ref,
        res_ref,
        ow_ref,
        gain_ref,
        normed_v,
        mixed_v,
        prepare,
        load_weights,
        kbuf,
        vbuf,
        kt,
        vext,
        qbuf,
        osend,
        orecv,
        ssend,
        srecv,
        att,
        ow_v,
        psend,
        precv,
        res_v,
        gain_v,
        in_sem,
        kv_send,
        kv_recv,
        q_send,
        q_recv,
        o_send,
        o_recv,
        s_send,
        s_recv,
        p_send,
        p_recv,
        ow_sem,
    )
    wd_copy = pltpu.make_async_copy(wd_ref, wd_v, wd_sem)
    wd_copy.start()
    expert_kernel(
        n_ctx,
        n_exp,
        chunks,
        waves,
        cap,
        w_copies,
        wd_copy,
        normed_v,
        out_ref,
        nbuf,
        sel_v,
        back_v,
        slot_gate,
        mixed_v,
        xall,
        wg_v,
        wu_v,
        wd_v,
        acc_g,
        acc_u,
        hid,
        tbuf,
        sbuf,
        dbuf,
        ybuf,
        xbuf,
        fbuf,
        wsend,
        wrecv,
        n_send,
        n_recv,
        a_send,
        a_recv,
        r_send,
        r_recv,
        e_send,
        e_recv,
    )
    drain()


def layer(limit, q, nk, nv, ck, cv, res, ow, gain, wg, wu, wd, ids, gates):
    n_ctx, n_exp = lax.axis_size("ctx"), lax.axis_size("exp")
    n_chip, n_y = n_ctx // 2, n_ctx // 4
    tok, q_width = q.shape
    cache = ck.shape[0]
    sub, width = res.shape
    rows = 2 * (cache + tok)
    block = (q_width // HD) * tok
    hidden = wg.shape[1]
    cap = 3 * tok // n_exp
    chunks, waves = 4, 3
    steps, part = chunks * waves, cap // waves
    span = width // chunks
    total = n_ctx * cap
    vmem = pl.BlockSpec(memory_space=pltpu.VMEM)
    hbm = pl.BlockSpec(memory_space=pl.ANY)
    dma = pltpu.SemaphoreType.DMA
    return pl.pallas_call(
        functools.partial(layer_kernel, n_ctx, n_exp, chunks, waves, cap),
        out_shape=jax.ShapeDtypeStruct((sub, width), BF16),
        in_specs=[pl.BlockSpec(memory_space=pltpu.SMEM)] + [hbm] * 11 + [vmem] * 2,
        out_specs=vmem,
        scratch_shapes=[
            pltpu.VMEM((rows, HD), BF16),
            pltpu.VMEM((rows, HD), BF16),
            pltpu.VMEM((HD, rows), BF16),
            pltpu.VMEM((rows, 2 * HD), BF16),
            pltpu.VMEM((n_chip, block, HD), BF16),
            pltpu.VMEM((n_chip, block, HD), BF16),
            pltpu.VMEM((n_chip, block, HD), BF16),
            pltpu.VMEM((n_chip, 8, tok), F32),
            pltpu.VMEM((n_chip, 8, tok), F32),
            pltpu.VMEM((tok, q_width), BF16),
            pltpu.VMEM((tok, width), BF16),
            pltpu.VMEM((n_exp, sub, width), BF16),
            pltpu.VMEM((sub, width), BF16),
            pltpu.VMEM((1, width), BF16),
            dma((q_width // HD + 6,)),
            dma((4,)),
            dma((4,)),
            dma,
            dma((n_chip,)),
            dma,
            dma,
            dma,
            dma,
            dma,
            dma((2,)),
            dma,
            pltpu.VMEM((sub, width), BF16),
            pltpu.VMEM((tok, width), BF16),
            pltpu.VMEM((cap, tok), BF16),
            pltpu.VMEM((tok, cap), BF16),
            pltpu.VMEM((cap, 1), F32),
            pltpu.VMEM((sub, width), F32),
            pltpu.VMEM((steps, 2, 2, n_y, part, span), BF16),
            pltpu.VMEM((width, hidden), BF16),
            pltpu.VMEM((width, hidden), BF16),
            pltpu.VMEM((hidden, width), BF16),
            pltpu.VMEM((total // waves, hidden), F32),
            pltpu.VMEM((total // waves, hidden), F32),
            pltpu.VMEM((total // waves, hidden), BF16),
            pltpu.VMEM((steps, 2, 2, n_y, part, span), BF16),
            pltpu.VMEM((steps, 2, n_y, part, span), BF16),
            pltpu.VMEM((cap, width), BF16),
            pltpu.VMEM((steps // 2, 3, 2, part, span), BF16),
            pltpu.VMEM((steps // 2, n_y, part, span), BF16),
            pltpu.VMEM((steps, 3, part, span), BF16),
            pltpu.VMEM((tok, width), BF16),
            pltpu.VMEM((n_exp, sub, width), BF16),
            dma,
            dma((chunks,)),
            dma((5,)),
            dma((4, steps)),
            dma((5,)),
            dma((5, steps)),
            dma,
            dma((chunks,)),
            dma((chunks,)),
            dma((chunks,)),
            dma,
        ],
        compiler_params=pltpu.CompilerParams(
            collective_id=0, has_side_effects=True, vmem_limit_bytes=60 * 2**20
        ),
        cost_estimate=pl.CostEstimate(
            flops=6 * total * width * hidden + 4 * n_chip * block * rows * HD,
            bytes_accessed=6 * width * hidden,
            transcendentals=total * hidden + n_chip * block * rows,
        ),
    )(limit, q, nk, nv, ck, cv, res, ow, gain, wg, wu, wd, ids, gates)


def local(
    queries,
    new_keys,
    new_values,
    cache_keys,
    cache_values,
    cache_length,
    residual,
    out_weight,
    norm_gain,
    route_ids,
    route_gates,
    w_gate,
    w_up,
    w_down,
):
    return layer(
        cache_length,
        queries,
        new_keys,
        new_values,
        cache_keys,
        cache_values,
        residual,
        out_weight,
        norm_gain[None, :],
        w_gate[0],
        w_up[0],
        w_down[0],
        route_ids.T,
        route_gates.T,
    )


def solution(mesh):
    placed = (
        P("ctx", "exp"),
        P("ctx", "exp"),
        P("ctx", "exp"),
        P("ctx", "exp"),
        P("ctx", "exp"),
        P(),
        P(("ctx", "exp"), None),
        P("exp", None),
        P(),
        P("ctx", None),
        P("ctx", None),
        P("exp", None, "ctx"),
        P("exp", None, "ctx"),
        P("exp", "ctx", None),
    )
    return jax.shard_map(
        local, mesh=mesh, in_specs=placed, out_specs=P(("ctx", "exp"), None), check_vma=False
    )
```

```python
import functools
import math

import jax
import jax.numpy as jnp
from jax import lax
from jax.experimental import pallas as pl
from jax.experimental.pallas import tpu as pltpu
from jax.sharding import PartitionSpec as P

HD = 128
NEG = -1e30
EPS = 1e-05
MESH = pl.DeviceIdType.MESH
F32 = jnp.float32
BF16 = jnp.bfloat16


def remote(src, dst, send, recv, where):
    return pltpu.make_async_remote_copy(
        src_ref=src,
        dst_ref=dst,
        send_sem=send,
        recv_sem=recv,
        device_id=where,
        device_id_type=MESH,
    )


def arrived(ref, sem):
    pltpu.make_async_copy(ref, ref, sem).wait()


def attend_kernel(
    n_ctx,
    n_exp,
    limit_ref,
    q_ref,
    nk_ref,
    nv_ref,
    ck_ref,
    cv_ref,
    res_ref,
    ow_ref,
    gain_ref,
    normed_ref,
    mixed_ref,
    prepare,
    load_weights,
    kbuf,
    vbuf,
    kt,
    vext,
    qbuf,
    osend,
    orecv,
    ssend,
    srecv,
    att,
    ow_v,
    psend,
    precv,
    res_v,
    gain_v,
    in_sem,
    kv_send,
    kv_recv,
    q_send,
    q_recv,
    o_send,
    o_recv,
    s_send,
    s_recv,
    p_send,
    p_recv,
    ow_sem,
):
    n_chip = n_ctx // 2
    me = lax.axis_index("ctx")
    ex = lax.axis_index("exp")
    chip = me // 2
    core = me % 2
    sib = me + 1 - 2 * core
    tok = q_ref.shape[0]
    group = q_ref.shape[1] // HD
    cache = ck_ref.shape[0]
    sub, width = res_ref.shape
    c_all = 2 * cache
    rows = c_all + 2 * tok

    ow_copy = pltpu.make_async_copy(ow_ref, ow_v, ow_sem)
    barrier = pltpu.get_barrier_semaphore()

    def greet_chip(s, _):
        peer = ((chip + s) % n_chip) * 2 + core
        pl.semaphore_signal(barrier, inc=1, device_id={"ctx": peer}, device_id_type=MESH)
        return 0

    def greet_exp(s, _):
        pl.semaphore_signal(
            barrier, inc=1, device_id={"exp": (ex + s) % n_exp}, device_id_type=MESH
        )
        return 0

    pl.semaphore_signal(barrier, inc=1, device_id={"ctx": sib}, device_id_type=MESH)
    lax.fori_loop(1, n_chip, greet_chip, 0)
    lax.fori_loop(1, n_exp, greet_exp, 0)

    moves = [
        (q_ref.at[:, pl.ds(g * HD, HD)], qbuf.at[chip, pl.ds(g * tok, tok)]) for g in range(group)
    ]
    moves += [
        (ck_ref, kbuf.at[pl.ds(0, cache)]),
        (nk_ref, kbuf.at[pl.ds(c_all, tok)]),
        (cv_ref, vbuf.at[pl.ds(0, cache)]),
        (nv_ref, vbuf.at[pl.ds(c_all, tok)]),
        (res_ref, res_v),
        (gain_ref, gain_v),
    ]
    loads = [pltpu.make_async_copy(a, b, in_sem.at[i]) for i, (a, b) in enumerate(moves)]
    for load in loads:
        load.start()
    for load in loads[0:group]:
        load.wait()
    prepare()
    pl.semaphore_wait(barrier, n_chip + n_exp - 1)

    kv_copies = [
        remote(src, dst, kv_send.at[i], kv_recv.at[i], {"ctx": sib})
        for i, (src, dst) in enumerate(
            [
                (ck_ref, kbuf.at[pl.ds(cache, cache)]),
                (nk_ref, kbuf.at[pl.ds(c_all + tok, tok)]),
                (cv_ref, vbuf.at[pl.ds(cache, cache)]),
                (nv_ref, vbuf.at[pl.ds(c_all + tok, tok)]),
            ]
        )
    ]
    for copy in kv_copies:
        copy.start()

    def q_copy(s):
        peer = ((chip + n_chip - s) % n_chip) * 2 + core
        return remote(
            qbuf.at[chip], qbuf.at[chip], q_send, q_recv.at[chip], {"ctx": peer}
        )

    def q_start(s, _):
        q_copy(s).start()
        return 0

    lax.fori_loop(1, n_chip, q_start, 0)
    ow_copy.start()
    load_weights()
    for load in loads[group:]:
        load.wait()

    for copy in kv_copies:
        copy.wait_recv()
    kt[...] = kbuf[...].T
    vext[:, 0:HD] = vbuf[...]
    vext[:, HD : 2 * HD] = jnp.ones((rows, HD), BF16)

    limit = limit_ref[0]
    position = lax.broadcasted_iota(jnp.int32, (1, cache), 1)
    bias_own = jnp.where(position + me * cache < limit, 0.0, NEG)
    bias_sib = jnp.where(position + sib * cache < limit, 0.0, NEG)
    cache_bias = jnp.concatenate([bias_own, bias_sib], axis=1)
    t_row = lax.broadcasted_iota(jnp.int32, (tok, 2 * tok), 0)
    t_col = lax.broadcasted_iota(jnp.int32, (tok, 2 * tok), 1)
    lane = lax.broadcasted_iota(jnp.int32, (tok, HD), 1)
    key_at = jnp.where(t_col < tok, t_col + me * tok, t_col - tok + sib * tok)
    scale = math.log2(math.e) / math.sqrt(HD)

    def o_copy(s, src):
        peer = src * 2 + core
        return (
            remote(osend.at[s], orecv.at[chip], o_send, o_recv, {"ctx": peer}),
            remote(ssend.at[s], srecv.at[chip], s_send, s_recv, {"ctx": peer}),
        )

    def step(s, _):
        src = (chip + s) % n_chip

        @pl.when(s > 0)
        def _():
            arrived(qbuf.at[src], q_recv.at[src])

        query_at = t_row + (src * 2 + core) * tok
        new_bias = jnp.where(key_at <= query_at, 0.0, NEG)
        stat = jnp.zeros((tok, HD), F32)
        for g in range(group):
            q = qbuf[src, g * tok : (g + 1) * tok, :]
            sc = jnp.dot(q, kt[:, 0:c_all], preferred_element_type=F32) * scale + cache_bias
            sn = jnp.dot(q, kt[:, c_all:rows], preferred_element_type=F32) * scale + new_bias
            top = jnp.maximum(
                jnp.max(sc, axis=1, keepdims=True), jnp.max(sn, axis=1, keepdims=True)
            )
            pc = jnp.exp2(sc - top).astype(BF16)
            pn = jnp.exp2(sn - top).astype(BF16)
            o = jnp.dot(pc, vext[0:c_all, :], preferred_element_type=F32) + jnp.dot(
                pn, vext[c_all:rows, :], preferred_element_type=F32
            )
            total = o[:, HD : 2 * HD]
            osend[s, g * tok : (g + 1) * tok, :] = (o[:, 0:HD] / total).astype(BF16)
            stat = jnp.where(lane == g, top + jnp.log2(total), stat)
        ssend[s] = stat.T[0:8, :]

        @pl.when(s > 0)
        def _():
            for copy in o_copy(s, src):
                copy.start()

        return 0

    lax.fori_loop(0, n_chip, step, 0)
    orecv[chip] = osend[0]
    srecv[chip] = ssend[0]

    arrived(orecv.at[pl.ds(0, n_chip - 1)], o_recv)
    arrived(srecv.at[pl.ds(0, n_chip - 1)], s_recv)

    stats = srecv[...]
    peak = jnp.max(stats, axis=0, keepdims=True)
    share = jnp.exp2(stats - peak)
    share = share / jnp.sum(share, axis=0, keepdims=True)
    share = share.reshape(n_chip * 8, tok)
    if n_chip * 8 < HD:
        share = jnp.concatenate([share, jnp.zeros((HD - n_chip * 8, tok), F32)], axis=0)
    share = share.T
    for g in range(group):
        value = jnp.zeros((tok, HD), F32)
        for i in range(n_chip):
            part = orecv[i, g * tok : (g + 1) * tok, :].astype(F32)
            value = value + share[:, i * 8 + g : i * 8 + g + 1] * part
        att[:, g * HD : (g + 1) * HD] = value.astype(BF16)

    ow_copy.wait()
    half = width // 2
    tile = min(512, half)

    def p_copy(h, s):
        peer = (ex + s) % n_exp
        columns = pl.ds(h * half, half)
        return remote(
            psend.at[pl.ds(pl.multiple_of(peer * sub, sub), sub), columns],
            precv.at[ex, :, columns],
            p_send,
            p_recv.at[h],
            {"exp": peer},
        )

    for h in range(2):

        def project(n, _, h=h):
            columns = pl.ds(pl.multiple_of(h * half + n * tile, tile), tile)
            psend[:, columns] = jnp.dot(
                att[...], ow_v[:, columns], preferred_element_type=F32
            ).astype(BF16)
            return 0

        lax.fori_loop(0, half // tile, project, 0)

        def p_start(s, _, h=h):
            p_copy(h, s).start()
            return 0

        lax.fori_loop(1, n_exp, p_start, 0)

    precv[ex] = psend[pl.ds(pl.multiple_of(ex * sub, sub), sub), :]
    for h in range(2):
        columns = pl.ds(h * half, half)

        arrived(psend.at[pl.ds(0, (n_exp - 1) * sub), columns], p_recv.at[h])
        value = res_v[:, columns].astype(F32)
        for j in range(n_exp):
            value = value + precv[j, :, columns].astype(F32)
        mixed_ref[:, columns] = value

    mixed = mixed_ref[...]
    square = jnp.mean(mixed * mixed, axis=1, keepdims=True)
    normed_ref[...] = (mixed * lax.rsqrt(square + EPS) * gain_v[...].reshape(1, width).astype(F32)).astype(BF16)

    def drain():
        for copy in kv_copies:
            copy.wait_send()
        arrived(qbuf.at[pl.ds(0, n_chip - 1)], q_send)
        arrived(osend.at[pl.ds(0, n_chip - 1)], o_send)
        arrived(ssend.at[pl.ds(0, n_chip - 1)], s_send)
        arrived(psend.at[pl.ds(0, (n_exp - 1) * sub)], p_send)

    return drain


def select_slots(ids_ref, gates_ref, sel_v, back_v, slot_gate):
    ex = lax.axis_index("exp")
    cap, tok = sel_v.shape
    slots = -(-cap // HD) * HD
    first, second = ids_ref[0:1, :] == ex, ids_ref[1:2, :] == ex
    hit = jnp.where(first, 1.0, 0.0) + jnp.where(second, 1.0, 0.0)
    weight = jnp.where(first, gates_ref[0:1, :], 0.0) + jnp.where(second, gates_ref[1:2, :], 0.0)
    earlier = lax.broadcasted_iota(jnp.int32, (tok, tok), 0) <= lax.broadcasted_iota(
        jnp.int32, (tok, tok), 1
    )
    count = jnp.dot(
        jnp.broadcast_to(hit, (16, tok)).astype(BF16),
        jnp.where(earlier, 1.0, 0.0).astype(BF16),
        preferred_element_type=F32,
    )
    place = lax.broadcasted_iota(jnp.int32, (slots, tok), 0).astype(F32)
    chosen = jnp.where(place == count[0:1, :] - 1.0, hit, 0.0)
    sel_v[...] = chosen[0:cap, :].astype(BF16)
    back_v[...] = chosen.T[:, 0:cap].astype(BF16)
    slot_gate[...] = jnp.sum(chosen * weight, axis=1, keepdims=True)[0:cap, :]


def expert_kernel(
    n_ctx,
    n_exp,
    chunks,
    waves,
    cap,
    w_copies,
    wd_copy,
    normed_ref,
    out_ref,
    nbuf,
    sel_v,
    back_v,
    slot_gate,
    mixed_v,
    xall,
    wg_v,
    wu_v,
    wd_v,
    acc_g,
    acc_u,
    hid,
    tbuf,
    sbuf,
    dbuf,
    ybuf,
    xbuf,
    fbuf,
    wsend,
    wrecv,
    n_send,
    n_recv,
    a_send,
    a_recv,
    r_send,
    r_recv,
    e_send,
    e_recv,
):
    n_y = n_ctx // 4
    me = lax.axis_index("ctx")
    ex = lax.axis_index("exp")
    k = me % 2
    x = me // (2 * n_y)
    y = (me // 2) % n_y
    y_up, y_down, y_far = (y + 1) % n_y, (y + n_y - 1) % n_y, (y + 2) % n_y
    sib = {"ctx": me + 1 - 2 * k}
    across = {"ctx": ((1 - x) * n_y + y) * 2 + k}
    up = {"ctx": (x * n_y + y_up) * 2 + k}
    down = {"ctx": (x * n_y + y_down) * 2 + k}
    far = {"ctx": (x * n_y + y_far) * 2 + k}
    sub, width = out_ref.shape
    tok = sub * n_exp
    total = n_ctx * cap
    part = cap // waves
    steps = waves * chunks
    span = width // chunks
    own_rows = pl.ds(pl.multiple_of(ex * sub, sub), sub)

    def cols(c):
        return pl.ds(pl.multiple_of(c * span, span), span)

    nbuf[own_rows, :] = normed_ref[...]

    def n_copy(c, s, row_of, peer):
        at = pl.ds(pl.multiple_of(row_of * sub, sub), sub)
        return remote(
            normed_ref.at[:, cols(c)],
            nbuf.at[at, cols(c)],
            n_send,
            n_recv.at[c],
            {"exp": peer},
        )

    def n_start(c, _):
        def one(s, _):
            n_copy(c, s, ex, (ex + s) % n_exp).start()
            return 0

        lax.fori_loop(1, n_exp, one, 0)
        return 0

    lax.fori_loop(0, chunks, n_start, 0)

    half = steps // 2

    def gather(kind, c, at, where):
        ref = xall.at[(c, *at)]
        return remote(ref, ref, a_send.at[kind], a_recv.at[min(kind, 3), c], where)

    def a_own(c):
        return [gather(0, c, (k, x, y), where) for where in (up, down, far)]

    def a_pass(c):
        return [gather(1, c, (k, 1 - x, y), where) for where in (up, down, far)]

    def a_block(c):
        return gather(2, c, (k, x, y), across)

    def a_plane(c):
        ref = xall.at[c, k, x]
        return remote(ref, ref, a_send.at[4], a_recv.at[2, c], across)

    def a_sib(c, plane):
        return gather(3, c, (k, plane), sib)

    three = pl.ds(0, 3)

    def reduce(kind, c, src, dst, where):
        return remote(src, dst, r_send.at[kind], r_recv.at[kind, c], where)

    def r_sib(c):
        return reduce(0, c, tbuf.at[c, 1 - k], sbuf.at[c], sib)

    def r_pairs(c):
        return (
            reduce(1, c, tbuf.at[c, k, :, y_up], ybuf.at[c // 2, 0], up),
            reduce(1, c, tbuf.at[c, k, :, y_down], ybuf.at[c // 2, 1], down),
            reduce(1, c, tbuf.at[c, k, :, y_far], ybuf.at[c // 2, 2], far),
        )

    def r_block(c):
        return reduce(2, c, tbuf.at[c, k, 1 - x, y], fbuf.at[c, 0], across)

    def r_plane(c):
        return reduce(3, c, tbuf.at[c, k, 1 - x], xbuf.at[c // 2], across)

    def r_own(c):
        return (
            reduce(4, c, tbuf.at[c, k, x, y_up], fbuf.at[c, 0], up),
            reduce(4, c, tbuf.at[c, k, x, y_down], fbuf.at[c, 1], down),
            reduce(4, c, tbuf.at[c, k, x, y_far], fbuf.at[c, 2], far),
        )

    def e_copy(c, s, row_of, slot, peer):
        at = pl.ds(pl.multiple_of(row_of * sub, sub), sub)
        return remote(
            wsend.at[at, cols(c)],
            wrecv.at[slot, :, cols(c)],
            e_send,
            e_recv.at[c],
            {"exp": peer},
        )

    def wave_rows(i):
        return pl.ds(pl.multiple_of(i // chunks * part, part), part)

    def step(it, _):
        @pl.when(it < chunks)
        def _():
            arrived(nbuf.at[pl.ds(0, (n_exp - 1) * sub), cols(it)], n_recv.at[it])

        @pl.when(it < steps)
        def _():
            i = it
            xall[i, k, x, y] = jnp.dot(
                sel_v[wave_rows(i), :], nbuf[:, cols(i % chunks)], preferred_element_type=F32
            ).astype(BF16)

            @pl.when(i % 2 == 0)
            def _():
                a_block(i).start()

            for copy in a_own(i):
                copy.start()

        @pl.when((it >= 3) & (it < steps + 3))
        def _():
            i = it - 3

            @pl.when(i % 2 == 0)
            def _():
                arrived(xall.at[i, k, 1 - x, y], a_recv.at[2, i])
                for copy in a_pass(i):
                    copy.start()
                arrived(xall.at[i, k, x, three], a_recv.at[0, i])

            @pl.when(i % 2 == 1)
            def _():
                arrived(xall.at[i, k, x, three], a_recv.at[0, i])
                a_plane(i).start()

            a_sib(i, x).start()

        @pl.when((it >= 6) & (it < steps + 6))
        def _():
            i = it - 6

            @pl.when(i % 2 == 0)
            def _():
                arrived(xall.at[i, k, 1 - x, three], a_recv.at[1, i])

            @pl.when(i % 2 == 1)
            def _():
                arrived(xall.at[i, k, 1 - x], a_recv.at[2, i])

            a_sib(i, 1 - x).start()

        r = it - (chunks + 7)

        @pl.when((r >= 1) & (r < steps + 1))
        def _():
            i = r - 1
            arrived(sbuf.at[i], r_recv.at[0, i])
            tbuf[i, k] = (tbuf[i, k].astype(F32) + sbuf[i].astype(F32)).astype(BF16)

            @pl.when(i % 2 == 0)
            def _():
                for copy in r_pairs(i):
                    copy.start()

            @pl.when(i % 2 == 1)
            def _():
                r_plane(i).start()

        @pl.when((r >= 4) & (r < steps + 4))
        def _():
            i = r - 4

            @pl.when(i % 2 == 0)
            def _():
                arrived(ybuf.at[i // 2], r_recv.at[1, i])
                for px in range(2):
                    value = tbuf[i, k, px, y].astype(F32)
                    for j in range(3):
                        value = value + ybuf[i // 2, j, px].astype(F32)
                    tbuf[i, k, px, y] = value.astype(BF16)
                r_block(i).start()

            @pl.when(i % 2 == 1)
            def _():
                arrived(xbuf.at[i // 2], r_recv.at[3, i])
                tbuf[i, k, x] = (tbuf[i, k, x].astype(F32) + xbuf[i // 2].astype(F32)).astype(BF16)
                for copy in r_own(i):
                    copy.start()

        @pl.when((r >= 7) & (r < steps + 7))
        def _():
            i = r - 7
            c = i % chunks

            @pl.when(i % 2 == 0)
            def _():
                arrived(fbuf.at[i, 0], r_recv.at[2, i])
                value = tbuf[i, k, x, y].astype(F32) + fbuf[i, 0].astype(F32)
                tbuf[i, k, x, y] = value.astype(BF16)

            @pl.when(i % 2 == 1)
            def _():
                arrived(fbuf.at[i], r_recv.at[4, i])
                value = tbuf[i, k, x, y].astype(F32)
                for j in range(3):
                    value = value + fbuf[i, j].astype(F32)
                tbuf[i, k, x, y] = value.astype(BF16)

            scaled = slot_gate[wave_rows(i), :] * tbuf[i, k, x, y].astype(F32)
            dbuf[wave_rows(i), cols(c)] = scaled.astype(BF16)

            @pl.when(i >= steps - chunks)
            def _():
                wsend[:, cols(c)] = jnp.dot(
                    back_v[...], dbuf[:, cols(c)], preferred_element_type=F32
                ).astype(BF16)

                def start(s, _):
                    peer = (ex + s) % n_exp
                    e_copy(c, s, peer, ex, peer).start()
                    return 0

                lax.fori_loop(1, n_exp, start, 0)
                wrecv[ex, :, cols(c)] = wsend[own_rows, cols(c)]

        @pl.when(r >= steps - chunks + 9)
        def _():
            c = (r - 9) % chunks
            arrived(wsend.at[pl.ds(0, (n_exp - 1) * sub), cols(c)], e_recv.at[c])
            value = mixed_v[:, cols(c)]
            for j in range(n_exp):
                value = value + wrecv[j, :, cols(c)].astype(F32)
            out_ref[:, cols(c)] = value.astype(BF16)

        @pl.when(r == 0)
        def _():
            wd_copy.wait()

        @pl.when((r >= 0) & (r < steps))
        def _():
            i = r
            tbuf[i] = (
                jnp.dot(hid[...], wd_v[:, cols(i % chunks)], preferred_element_type=F32)
                .astype(BF16)
                .reshape(2, 2, n_y, part, span)
            )
            r_sib(i).start()

        @pl.when((it >= 7) & (it < chunks + 7))
        def _():
            for copy in w_copies(it - 7):
                copy.wait()

        @pl.when((it >= 7) & (it < steps + 7))
        def _():
            i = it - 7
            c = i % chunks
            arrived(xall.at[i, 1 - k], a_recv.at[3, i])

            @pl.when(c == 0)
            def _():
                acc_g[...] = jnp.zeros_like(acc_g)
                acc_u[...] = jnp.zeros_like(acc_u)

            lhs = xall[i].reshape(total // waves, span)
            acc_g[...] += jnp.dot(lhs, wg_v[cols(c), :], preferred_element_type=F32)
            acc_u[...] += jnp.dot(lhs, wu_v[cols(c), :], preferred_element_type=F32)

            @pl.when(c == chunks - 1)
            def _():
                gate = acc_g[...]
                hid[...] = (gate / (1.0 + jnp.exp(-gate)) * acc_u[...]).astype(BF16)

        return 0

    lax.fori_loop(0, steps + chunks + 16, step, 0)

    few = pl.ds(0, half)
    for i, ref in enumerate(
        [
            xall.at[:, 0, 0, three],
            xall.at[few, 0, 0, three],
            xall.at[few, 0, 0, 0],
            xall.at[:, 0],
            xall.at[few, 0, 0],
        ]
    ):
        arrived(ref, a_send.at[i])
    for i, ref in enumerate([sbuf, ybuf, fbuf.at[few, 0], xbuf, fbuf.at[few]]):
        arrived(ref, r_send.at[i])
    others = pl.ds(0, (n_exp - 1) * sub)
    arrived(nbuf.at[others], n_send)
    arrived(wsend.at[others], e_send)


def layer_kernel(
    n_ctx,
    n_exp,
    chunks,
    waves,
    cap,
    limit_ref,
    q_ref,
    nk_ref,
    nv_ref,
    ck_ref,
    cv_ref,
    res_ref,
    ow_ref,
    gain_ref,
    wg_ref,
    wu_ref,
    wd_ref,
    ids_ref,
    gates_ref,
    out_ref,
    kbuf,
    vbuf,
    kt,
    vext,
    qbuf,
    osend,
    orecv,
    ssend,
    srecv,
    att,
    psend,
    precv,
    res_v,
    gain_v,
    in_sem,
    kv_send,
    kv_recv,
    q_send,
    q_recv,
    o_send,
    o_recv,
    s_send,
    s_recv,
    p_send,
    p_recv,
    ow_sem,
    normed_v,
    nbuf,
    sel_v,
    back_v,
    slot_gate,
    mixed_v,
    xall,
    wg_v,
    wu_v,
    wd_v,
    acc_g,
    acc_u,
    hid,
    tbuf,
    sbuf,
    dbuf,
    ybuf,
    xbuf,
    fbuf,
    wsend,
    wrecv,
    n_send,
    n_recv,
    a_send,
    a_recv,
    r_send,
    r_recv,
    e_send,
    e_recv,
    wg_sem,
    wu_sem,
    wd_sem,
):
    span = wg_ref.shape[0] // chunks

    def w_copies(c):
        at = pl.ds(pl.multiple_of(c * span, span), span)
        return (
            pltpu.make_async_copy(wg_ref.at[at], wg_v.at[at], wg_sem.at[c]),
            pltpu.make_async_copy(wu_ref.at[at], wu_v.at[at], wu_sem.at[c]),
        )

    def load_weights():
        def one(c, _):
            for copy in w_copies(c):
                copy.start()
            return 0

        lax.fori_loop(0, chunks, one, 0)

    def prepare():
        select_slots(ids_ref, gates_ref, sel_v, back_v, slot_gate)

    ow_v = wd_v.at[pl.ds(0, ow_ref.shape[0])]
    drain = attend_kernel(
        n_ctx,
        n_exp,
        limit_ref,
        q_ref,
        nk_ref,
        nv_ref,
        ck_ref,
        cv_ref,
        res_ref,
        ow_ref,
        gain_ref,
        normed_v,
        mixed_v,
        prepare,
        load_weights,
        kbuf,
        vbuf,
        kt,
        vext,
        qbuf,
        osend,
        orecv,
        ssend,
        srecv,
        att,
        ow_v,
        psend,
        precv,
        res_v,
        gain_v,
        in_sem,
        kv_send,
        kv_recv,
        q_send,
        q_recv,
        o_send,
        o_recv,
        s_send,
        s_recv,
        p_send,
        p_recv,
        ow_sem,
    )
    wd_copy = pltpu.make_async_copy(wd_ref, wd_v, wd_sem)
    wd_copy.start()
    expert_kernel(
        n_ctx,
        n_exp,
        chunks,
        waves,
        cap,
        w_copies,
        wd_copy,
        normed_v,
        out_ref,
        nbuf,
        sel_v,
        back_v,
        slot_gate,
        mixed_v,
        xall,
        wg_v,
        wu_v,
        wd_v,
        acc_g,
        acc_u,
        hid,
        tbuf,
        sbuf,
        dbuf,
        ybuf,
        xbuf,
        fbuf,
        wsend,
        wrecv,
        n_send,
        n_recv,
        a_send,
        a_recv,
        r_send,
        r_recv,
        e_send,
        e_recv,
    )
    drain()


def layer(limit, q, nk, nv, ck, cv, res, ow, gain, wg, wu, wd, ids, gates):
    n_ctx, n_exp = lax.axis_size("ctx"), lax.axis_size("exp")
    n_chip, n_y = n_ctx // 2, n_ctx // 4
    tok, q_width = q.shape
    cache = ck.shape[0]
    sub, width = res.shape
    rows = 2 * (cache + tok)
    block = (q_width // HD) * tok
    hidden = wg.shape[1]
    cap = 3 * tok // n_exp
    chunks, waves = 4, 3
    steps, part = chunks * waves, cap // waves
    span = width // chunks
    total = n_ctx * cap
    vmem = pl.BlockSpec(memory_space=pltpu.VMEM)
    hbm = pl.BlockSpec(memory_space=pl.ANY)
    dma = pltpu.SemaphoreType.DMA
    return pl.pallas_call(
        functools.partial(layer_kernel, n_ctx, n_exp, chunks, waves, cap),
        out_shape=jax.ShapeDtypeStruct((sub, width), BF16),
        in_specs=[pl.BlockSpec(memory_space=pltpu.SMEM)] + [hbm] * 11 + [vmem] * 2,
        out_specs=vmem,
        scratch_shapes=[
            pltpu.VMEM((rows, HD), BF16),
            pltpu.VMEM((rows, HD), BF16),
            pltpu.VMEM((HD, rows), BF16),
            pltpu.VMEM((rows, 2 * HD), BF16),
            pltpu.VMEM((n_chip, block, HD), BF16),
            pltpu.VMEM((n_chip, block, HD), BF16),
            pltpu.VMEM((n_chip, block, HD), BF16),
            pltpu.VMEM((n_chip, 8, tok), F32),
            pltpu.VMEM((n_chip, 8, tok), F32),
            pltpu.VMEM((tok, q_width), BF16),
            pltpu.VMEM((tok, width), BF16),
            pltpu.VMEM((n_exp, sub, width), BF16),
            pltpu.VMEM((sub, width), BF16),
            pltpu.VMEM((width,), BF16),
            dma((q_width // HD + 6,)),
            dma((4,)),
            dma((4,)),
            dma,
            dma((n_chip,)),
            dma,
            dma,
            dma,
            dma,
            dma,
            dma((2,)),
            dma,
            pltpu.VMEM((sub, width), BF16),
            pltpu.VMEM((tok, width), BF16),
            pltpu.VMEM((cap, tok), BF16),
            pltpu.VMEM((tok, cap), BF16),
            pltpu.VMEM((cap, 1), F32),
            pltpu.VMEM((sub, width), F32),
            pltpu.VMEM((steps, 2, 2, n_y, part, span), BF16),
            pltpu.VMEM((width, hidden), BF16),
            pltpu.VMEM((width, hidden), BF16),
            pltpu.VMEM((hidden, width), BF16),
            pltpu.VMEM((total // waves, hidden), F32),
            pltpu.VMEM((total // waves, hidden), F32),
            pltpu.VMEM((total // waves, hidden), BF16),
            pltpu.VMEM((steps, 2, 2, n_y, part, span), BF16),
            pltpu.VMEM((steps, 2, n_y, part, span), BF16),
            pltpu.VMEM((cap, width), BF16),
            pltpu.VMEM((steps // 2, 3, 2, part, span), BF16),
            pltpu.VMEM((steps // 2, n_y, part, span), BF16),
            pltpu.VMEM((steps, 3, part, span), BF16),
            pltpu.VMEM((tok, width), BF16),
            pltpu.VMEM((n_exp, sub, width), BF16),
            dma,
            dma((chunks,)),
            dma((5,)),
            dma((4, steps)),
            dma((5,)),
            dma((5, steps)),
            dma,
            dma((chunks,)),
            dma((chunks,)),
            dma((chunks,)),
            dma,
        ],
        compiler_params=pltpu.CompilerParams(
            collective_id=0, has_side_effects=True, vmem_limit_bytes=60 * 2**20
        ),
        cost_estimate=pl.CostEstimate(
            flops=6 * total * width * hidden + 4 * n_chip * block * rows * HD,
            bytes_accessed=6 * width * hidden,
            transcendentals=total * hidden + n_chip * block * rows,
        ),
    )(limit, q, nk, nv, ck, cv, res, ow, gain, wg, wu, wd, ids, gates)


def local(
    queries,
    new_keys,
    new_values,
    cache_keys,
    cache_values,
    cache_length,
    residual,
    out_weight,
    norm_gain,
    route_ids,
    route_gates,
    w_gate,
    w_up,
    w_down,
):
    return layer(
        cache_length,
        queries,
        new_keys,
        new_values,
        cache_keys,
        cache_values,
        residual,
        out_weight,
        norm_gain,
        w_gate[0],
        w_up[0],
        w_down[0],
        route_ids.T,
        route_gates.T,
    )


def solution(mesh):
    placed = (
        P("ctx", "exp"),
        P("ctx", "exp"),
        P("ctx", "exp"),
        P("ctx", "exp"),
        P("ctx", "exp"),
        P(),
        P(("ctx", "exp"), None),
        P("exp", None),
        P(),
        P("ctx", None),
        P("ctx", None),
        P("exp", None, "ctx"),
        P("exp", None, "ctx"),
        P("exp", "ctx", None),
    )
    return jax.shard_map(
        local, mesh=mesh, in_specs=placed, out_specs=P(("ctx", "exp"), None), check_vma=False
    )
```
